512 devices in a mesh: ctx: 64 (over z_lo, y, core), head: 8 (over x, z_hi).
Axes of the slice: x: 4, y: 4, z: 16 (z_hi: 2, z_lo: 8; z = z_hi * 8 + z_lo), core: 2. Of those that a mesh axis runs over, the one named last changes fastest.
Arguments:
- query_states: bfloat16 [8192, 2048], P('ctx', 'head'), may hold values from -40 to 40
- key_states: bfloat16 [8192, 1024], P('ctx', 'head'), may hold values from -5 to 5
- value_states: bfloat16 [8192, 1024], P('ctx', 'head'), may hold values from -6 to 6
- out_weight: bfloat16 [4096, 2048], P(None, 'head'), may hold values from -0.125 to 0.125
- out_grad: bfloat16 [8192, 4096], P('ctx', 'head'), may hold values from -6 to 6
- doc_lengths: int32 [16], replicated, may hold values from 1 to 4096, 8192 in all
- block_order: int32 [128], replicated, may hold values from 0 to 127, each once
Outputs:
- projected: bfloat16 [8192, 4096], P('ctx', 'head')
- grad_query: bfloat16 [8192, 2048], P('ctx', 'head')
- grad_key: bfloat16 [8192, 1024], P('ctx', 'head')
- grad_value: bfloat16 [8192, 1024], P('ctx', 'head')
The draws below stay inside these ranges and needn't reach their ends.
Inputs may be any that keep to these rules, and one draw needn't show every extreme that they name: `doc_lengths`: the lengths sum to 8192 and the longest is exactly 4096. `block_order`: each block number appears exactly once.
All inputs are finite; a program needn't handle non-finite values.
Results may differ from the reference program's by a relative error of at most 0.034.
Values may be sent and summed in bfloat16 or wider, within the bound.
No kernel may reach another device: no remote copies, remote signals or barrier semaphores. Data moves between devices by JAX's collectives and lax.ppermute only.
A program may use at most 64 MiB of HBM per device.

```python
import math
import jax
import jax.numpy as jnp
import numpy as np
from jax import lax

D = 4096
KVH = 8
HD = 128
QH = 16
BLOCK = 64
NDOC = 16
TOKENS = 8192
NBLK = 128
DOC_MAX = 4096


def draw_key_states(key, part):
    key = jax.random.fold_in(key, 3)
    return jnp.clip(jax.random.normal(key, (TOKENS, KVH * HD), jnp.float32), -5.0, 5.0).astype(jnp.bfloat16)


def draw_query_states(key, part):
    key = jax.random.fold_in(key, 4)
    return (2.0 * jnp.clip(jax.random.normal(key, (TOKENS, QH * HD), jnp.float32), -5.0, 5.0)).astype(jnp.bfloat16)


def level_of(own_key, extent, shards, low, top_value):
    loudness, own = 1.0, jax.random.fold_in(own_key, 6)
    for axis_at, blocks in shards:
        draws = jnp.exp(jax.random.uniform(jax.random.fold_in(own, axis_at), (blocks,), jnp.float32, low / len(shards), top_value / len(shards)))
        loudness = loudness * jnp.repeat(draws, extent[axis_at] // blocks).reshape([-1 if axis == axis_at else 1 for axis in range(len(extent))])
    return loudness


def profile(amount, total, limit, skew):
    weights = [(1 << 20) // math.isqrt(grade ** skew) + 1 for grade in range(2, amount + 1)]
    spare, counts = total - limit - (amount - 1), [1] * (amount - 1)
    while spare > 0:
        candidates = [i for i in range(amount - 1) if counts[i] < limit]
        mass, remaining = sum([weights[i] for i in candidates]), spare
        for i in candidates:
            more = min(limit - counts[i], max(1, remaining * weights[i] // mass), spare)
            counts[i] = counts[i] + more
            spare = spare - more
    return np.array([limit] + counts)


def ragged_sizes(key, amount, total, limit, slope):
    if amount == 2:
        one = jax.random.randint(key, (), max(1, total - limit), min(limit, total - 1) + 1)
        return jnp.stack([one, total - one])
    tallies = jnp.asarray(profile(amount, total, limit, slope), jnp.int32)
    twos = (amount - 1) // 2
    source_of, sink = tallies[1:1 + 2 * twos:2], tallies[2:2 + 2 * twos:2]
    room = jnp.minimum(source_of - 1, limit - sink)
    passed = jax.random.randint(jax.random.fold_in(key, 1), (twos,), 0, 1 << 20) % (room + 1)
    tallies = tallies.at[1:1 + 2 * twos:2].set(source_of - passed).at[2:2 + 2 * twos:2].set(sink + passed)
    return tallies[jax.random.permutation(jax.random.fold_in(key, 2), amount)]


def noise(key, extent, deviation, bound, split=(), held_as=jnp.bfloat16):
    values = deviation * jax.random.normal(key, extent, jnp.float32)
    if split:
        values = values * level_of(key, extent, split, -0.22, 0.18)
    return jnp.clip(values, -bound, bound).astype(held_as)


def setup_inputs(seed: int = 0) -> dict:
    seeds = jax.random.split(jax.random.key(seed), 8)
    query_states = draw_query_states(jax.random.fold_in(seeds[7], 71), 0)
    key_states = draw_key_states(jax.random.fold_in(seeds[7], 71), 0)
    value_states = noise(seeds[2], (TOKENS, KVH * HD), 1.0, 6.0, ((0, 64), (1, 8)))
    out_weight = noise(seeds[3], (D, QH * HD), (QH * HD) ** -0.5, 0.125, ((1, 8),))
    out_grad = noise(seeds[4], (TOKENS, D), 1.0, 6.0, ((0, 64), (1, 8)))
    doc_lengths = ragged_sizes(seeds[5], NDOC, TOKENS, DOC_MAX, 2).astype(jnp.int32)
    block_order = jax.random.permutation(seeds[6], NBLK).astype(jnp.int32)
    return dict(query_states=query_states, key_states=key_states, value_states=value_states, out_weight=out_weight, out_grad=out_grad, doc_lengths=doc_lengths, block_order=block_order)


NEGATIVE = -1.0e30


def rounded(values):
    return lax.optimization_barrier(values.astype(jnp.bfloat16)).astype(jnp.float32)


def reference(query_states, key_states, value_states, out_weight, out_grad, doc_lengths, block_order):
    total_rows = query_states.shape[0]
    group_size = QH // KVH
    score_scale = HD ** -0.5
    within = jnp.arange(BLOCK, dtype=jnp.int32)
    positions = (block_order[:, None] * BLOCK + within[None, :]).reshape(total_rows).astype(jnp.int32)
    doc_ends = jnp.cumsum(doc_lengths).astype(jnp.int32)
    documents = jnp.sum((positions[:, None] >= doc_ends[None, :]).astype(jnp.int32), axis=1)
    keys_whole = key_states.astype(jnp.float32).reshape(total_rows, KVH, HD)
    values_whole = value_states.astype(jnp.float32).reshape(total_rows, KVH, HD)
    queries_whole = query_states.astype(jnp.float32).reshape(total_rows, KVH, group_size, HD)
    block_rows = math.gcd(256, total_rows)
    block_starts = jnp.arange(total_rows // block_rows, dtype=jnp.int32) * block_rows

    def scores_for(first_row):
        queries_block = lax.dynamic_slice_in_dim(queries_whole, first_row, block_rows, 0)
        pos_block = lax.dynamic_slice_in_dim(positions, first_row, block_rows, 0)
        doc_block = lax.dynamic_slice_in_dim(documents, first_row, block_rows, 0)
        allowed = (doc_block[:, None] == documents[None, :]) & (positions[None, :] <= pos_block[:, None])
        scores = jnp.einsum("rkgd,nkd->kgrn", queries_block, keys_whole) * score_scale
        return queries_block, allowed, jnp.where(allowed, scores, NEGATIVE)

    def forward_block(first_row):
        queries_block, allowed, scores = scores_for(first_row)
        row_max = jnp.max(scores, axis=-1)
        weights = jnp.where(allowed, jnp.exp(scores - row_max[..., None]), 0.0)
        row_sum = jnp.sum(weights, axis=-1)
        blended = jnp.einsum("kgrn,nkd->kgrd", rounded(weights), values_whole) / row_sum[..., None]
        attn_block = blended.transpose(2, 0, 1, 3).reshape(block_rows, QH * HD).astype(jnp.bfloat16)
        return attn_block, row_max + jnp.log(row_sum)

    attn_blocks, sum_blocks = lax.map(forward_block, block_starts)
    attn_out = attn_blocks.reshape(total_rows, QH * HD)
    log_sums = sum_blocks.transpose(1, 2, 0, 3).reshape(KVH, group_size, total_rows)
    projected = jnp.dot(attn_out, out_weight.T, preferred_element_type=jnp.float32).astype(jnp.bfloat16)
    grad_attn = jnp.dot(out_grad, out_weight, preferred_element_type=jnp.float32).astype(jnp.bfloat16)
    grads_whole = grad_attn.astype(jnp.float32).reshape(total_rows, KVH, group_size, HD)
    attn_whole = attn_out.astype(jnp.float32).reshape(total_rows, KVH, group_size, HD)
    row_dots = jnp.sum(grads_whole * attn_whole, axis=-1).transpose(1, 2, 0)

    def backward_block(carried, first_row):
        grad_keys, grad_values = carried
        queries_block, allowed, scores = scores_for(first_row)
        grads_block = lax.dynamic_slice_in_dim(grads_whole, first_row, block_rows, 0)
        sums_block = lax.dynamic_slice_in_dim(log_sums, first_row, block_rows, 2)
        dots_block = lax.dynamic_slice_in_dim(row_dots, first_row, block_rows, 2)
        normed = jnp.where(allowed, jnp.exp(scores - sums_block[..., None]), 0.0)
        grad_values = grad_values + jnp.einsum("kgrn,rkgd->nkd", rounded(normed), grads_block)
        grad_probs = jnp.einsum("rkgd,nkd->kgrn", grads_block, values_whole)
        grad_scores = rounded(normed * (grad_probs - dots_block[..., None]))
        query_part = jnp.einsum("kgrn,nkd->rkgd", grad_scores, keys_whole) * score_scale
        grad_keys = grad_keys + jnp.einsum("kgrn,rkgd->nkd", grad_scores, queries_block)
        return (grad_keys, grad_values), query_part.reshape(block_rows, QH * HD).astype(jnp.bfloat16)

    empty_grads = jnp.zeros((total_rows, KVH, HD), jnp.float32)
    (grad_keys, grad_values), query_blocks = lax.scan(backward_block, (empty_grads, empty_grads), block_starts)
    grad_query = query_blocks.reshape(total_rows, QH * HD)
    grad_key = (grad_keys * score_scale).reshape(total_rows, KVH * HD).astype(jnp.bfloat16)
    grad_value = grad_values.reshape(total_rows, KVH * HD).astype(jnp.bfloat16)
    return (projected, grad_query, grad_key, grad_value)
```

```python
import functools
import math

import jax
import jax.numpy as jnp
from jax import lax
from jax.experimental import pallas as pl
from jax.experimental.pallas import tpu as pltpu
from jax.sharding import Mesh
from jax.sharding import PartitionSpec as P

HD = 128
BLOCK = 64
ROWS = 128
WIDE = 2 * HD
EXTRA = 16
CHUNK = 256
CHUNKS = 8
DOCS = 16
NEGATIVE = -1e30
SCALE = HD ** (-0.5)
SCALE2 = SCALE * math.log2(math.e)
VMEM = 40 * 1024 * 1024

NT = (((1,), (1,)), ((), ()))
NN = (((1,), (0,)), ((), ()))


def mm(a, b, dims):
    return lax.dot_general(a, b, dims, preferred_element_type=jnp.float32)


def heads_down(x):
    return jnp.concatenate([x[:, :HD], x[:, HD:]], axis=0)


def heads_across(x):
    return jnp.concatenate([x[:ROWS], x[ROWS:]], axis=1)


def split3(x):
    hi = x.astype(jnp.bfloat16)
    rest = x - hi.astype(jnp.float32)
    mid = rest.astype(jnp.bfloat16)
    low = (rest - mid.astype(jnp.float32)).astype(jnp.bfloat16)
    return hi, mid, low


def join3(rows, at):
    return rows[at : at + 1] + rows[at + 1 : at + 2] + rows[at + 2 : at + 3]


def query_rows(at_ref, order_ref, lengths_ref, t):
    z_lo, core = at_ref[0], at_ref[2]
    ctx = (z_lo * 4 + t) * 2 + core
    lane = lax.broadcasted_iota(jnp.int32, (1, WIDE), 1)
    row = lax.rem(lane, ROWS)
    first, second = order_ref[2 * ctx] * BLOCK, order_ref[2 * ctx + 1] * BLOCK
    pos = jnp.where(row < BLOCK, first + row, second + row - BLOCK)
    start = jnp.zeros_like(pos)
    end = 0
    for d in range(DOCS):
        end = end + lengths_ref[d]
        start = jnp.where(pos >= end, end, start)
    return pos, start


def key_base(at_ref, order_ref, block):
    z_lo, y, core = at_ref[0], at_ref[1], at_ref[2]
    part, z10, half = block // 8, (block // 2) % 4, block % 2
    z2 = z_lo // 4
    z2 = (1 - z2) if part % 2 else z2
    core = (1 - core) if part // 2 else core
    ctx = ((z2 * 4 + z10) * 4 + y) * 2 + core
    return order_ref[2 * ctx + half] * BLOCK


def allowed(pos, start, base):
    row = lax.broadcasted_iota(jnp.int32, (BLOCK, WIDE), 0)
    return (row >= start - base) & (row <= pos - base)


def kv_chunk(kv_refs, c, which):
    ref = kv_refs[c // 2]
    first = 2 * (c % 2)
    columns = slice(which * HD, (which + 1) * HD)
    return jnp.concatenate([ref[first, :, columns], ref[first + 1, :, columns]], axis=0)


def forward_kernel(
    at_ref, order_ref, lengths_ref, q_ref, kv0, kv1, kv2, kv3, out_ref, scores, v_t
):
    kv_refs = (kv0, kv1, kv2, kv3)
    for c in range(CHUNKS):
        v_t[:, c * CHUNK : (c + 1) * CHUNK] = kv_chunk(kv_refs, c, 1).T

    def tile(t, carried):
        queries = heads_down(q_ref[t])
        pos, start = query_rows(at_ref, order_ref, lengths_ref, t)
        top = jnp.full((1, WIDE), NEGATIVE, jnp.float32)
        for c in range(CHUNKS):
            s = mm(kv_chunk(kv_refs, c, 0), queries, NT)
            for b in range(CHUNK // BLOCK):
                base = key_base(at_ref, order_ref, c * 4 + b)
                part = jnp.where(
                    allowed(pos, start, base), s[b * BLOCK : (b + 1) * BLOCK], NEGATIVE
                )
                scores[pl.ds(c * CHUNK + b * BLOCK, BLOCK), :] = part
                top = jnp.maximum(top, jnp.max(part, axis=0, keepdims=True))
        top = jnp.maximum(top, 0.1 * NEGATIVE)
        total = jnp.zeros((1, WIDE), jnp.float32)
        acc = jnp.zeros((HD, WIDE), jnp.float32)
        for c in range(CHUNKS):
            e = jnp.exp2((scores[pl.ds(c * CHUNK, CHUNK), :] - top) * SCALE2)
            total = total + jnp.sum(e, axis=0, keepdims=True)
            acc = acc + mm(v_t[:, c * CHUNK : (c + 1) * CHUNK], e.astype(jnp.bfloat16), NN)
        some = total > 0
        safe = jnp.where(some, total, 1.0)
        out = (acc * (1.0 / safe)).T
        out_ref[t, :ROWS, :] = heads_across(out).astype(jnp.bfloat16)
        log_sum = jnp.where(some, top * SCALE2 + jnp.log2(safe), NEGATIVE)
        pad = jnp.zeros((EXTRA - 3, WIDE), jnp.float32)
        hi, mid, low = (v.astype(jnp.float32) for v in split3(log_sum))
        out_ref[t, ROWS:, :] = jnp.concatenate([hi, mid, low, pad], axis=0).astype(jnp.bfloat16)
        return carried

    lax.fori_loop(0, 4, tile, 0)


def combine_kernel(parts_ref, grad_ref, attn_ref, send_ref):
    sums = [join3(parts_ref[j, ROWS:, :].astype(jnp.float32), 0) for j in range(4)]
    top = functools.reduce(jnp.maximum, sums)
    weights = [jnp.exp2(s - top) for s in sums]
    total = functools.reduce(jnp.add, weights)
    log_sum = top + jnp.log2(total)
    inverse = 1.0 / total
    flat = []
    for w in weights:
        w = w * inverse
        flat += [w[:, :HD], w[:, HD:]]
    columns = jnp.concatenate(flat + [jnp.zeros((HD - 8, HD), jnp.float32)], axis=0).T
    halves, dots = [], []
    for h in range(2):
        lanes = slice(h * HD, (h + 1) * HD)
        acc = jnp.zeros((ROWS, HD), jnp.float32)
        for j in range(4):
            acc = acc + columns[:, 2 * j + h : 2 * j + h + 1] * parts_ref[
                j, :ROWS, lanes
            ].astype(jnp.float32)
        half = acc.astype(jnp.bfloat16)
        halves.append(half)
        dot = jnp.sum(
            half.astype(jnp.float32) * grad_ref[:, lanes].astype(jnp.float32),
            axis=1,
            keepdims=True,
        )
        dots.append(jnp.broadcast_to(dot, (ROWS, HD)).T[0:1])
    attn_ref[...] = jnp.concatenate(halves, axis=1)
    row_dots = jnp.concatenate(dots, axis=1)
    rows = [v.astype(jnp.float32) for v in split3(log_sum) + split3(row_dots)]
    extra = jnp.concatenate(rows + [jnp.zeros((EXTRA - 6, WIDE), jnp.float32)], axis=0)
    for j in range(4):
        send_ref[j, :ROWS, :] = grad_ref[...]
        send_ref[j, ROWS:, :] = extra.astype(jnp.bfloat16)


def backward_kernel(
    at_ref,
    order_ref,
    lengths_ref,
    q_ref,
    grad_ref,
    kv0,
    kv1,
    kv2,
    kv3,
    dq_ref,
    own_ref,
    far_ref,
    dk_acc,
    dv_acc,
    k_t,
):
    kv_refs = (kv0, kv1, kv2, kv3)
    for c in range(CHUNKS):
        k_t[:, c * CHUNK : (c + 1) * CHUNK] = kv_chunk(kv_refs, c, 0).T
    dk_acc[...] = jnp.zeros_like(dk_acc)
    dv_acc[...] = jnp.zeros_like(dv_acc)

    def tile(t, carried):
        queries = heads_down(q_ref[t])
        grads = heads_down(grad_ref[t, :ROWS, :])
        extra = grad_ref[t, ROWS:, :].astype(jnp.float32)
        log_sum, row_dots = join3(extra, 0), join3(extra, 3)
        pos, start = query_rows(at_ref, order_ref, lengths_ref, t)
        dq = jnp.zeros((HD, WIDE), jnp.float32)
        for c in range(CHUNKS):
            rows = pl.ds(c * CHUNK, CHUNK)
            s = mm(kv_chunk(kv_refs, c, 0), queries, NT)
            dp = mm(kv_chunk(kv_refs, c, 1), grads, NT)
            parts = []
            for b in range(CHUNK // BLOCK):
                base = key_base(at_ref, order_ref, c * 4 + b)
                raised = jnp.exp2(s[b * BLOCK : (b + 1) * BLOCK] * SCALE2 - log_sum)
                parts.append(jnp.where(allowed(pos, start, base), raised, 0.0))
            p = jnp.concatenate(parts, axis=0)
            ds = (p * (dp - row_dots)).astype(jnp.bfloat16)
            dv_acc[rows, :] += mm(p.astype(jnp.bfloat16), grads, NN)
            dk_acc[rows, :] += mm(ds, queries, NN)
            dq = dq + mm(k_t[:, c * CHUNK : (c + 1) * CHUNK], ds, NN)
        dq_ref[t] = heads_across((dq * SCALE).T).astype(jnp.bfloat16)
        return carried

    lax.fori_loop(0, 4, tile, 0)
    for part in range(4):
        ref = far_ref if part // 2 else own_ref
        for z10 in range(4):
            rows = pl.ds((part * 4 + z10) * ROWS, ROWS)
            ref[z10, part % 2, :, :HD] = (dk_acc[rows, :] * SCALE).astype(jnp.bfloat16)
            ref[z10, part % 2, :, HD:] = dv_acc[rows, :].astype(jnp.bfloat16)


def call(kernel, outs, scratch, smem, vmem, flops):
    specs = [pl.BlockSpec(memory_space=pltpu.SMEM)] * len(smem)
    specs += [pl.BlockSpec(memory_space=pltpu.VMEM)] * len(vmem)
    out_specs = [pl.BlockSpec(memory_space=pltpu.VMEM)] * len(outs)
    return pl.pallas_call(
        kernel,
        out_shape=[jax.ShapeDtypeStruct(o, jnp.bfloat16) for o in outs],
        in_specs=specs,
        out_specs=out_specs,
        scratch_shapes=scratch,
        compiler_params=pltpu.CompilerParams(vmem_limit_bytes=VMEM),
        cost_estimate=pl.CostEstimate(flops=flops, bytes_accessed=1 << 21, transcendentals=1 << 21),
    )(*smem, *vmem)


def spread(x, axis, n):
    return lax.all_to_all(jnp.broadcast_to(x, (n,) + x.shape), axis, 0, 0)


def swap(x, axis):
    return lax.ppermute(x, axis, [(0, 1), (1, 0)])


def per_device(
    query_states, key_states, value_states, out_weight, out_grad, doc_lengths, block_order
):
    z_hi = lax.axis_index("z_hi")
    z_lo = lax.axis_index("z2") * 4 + lax.axis_index("z10")
    at = jnp.stack([z_lo, lax.axis_index("y"), lax.axis_index("core")]).astype(jnp.int32)
    smem = (at, block_order, doc_lengths)

    other_grad = swap(out_grad, "z_hi")
    kv = jnp.concatenate([key_states, value_states], axis=1)
    kv_near = spread(kv, "z10", 4)
    kv_far = swap(kv_near, "z2")
    kv_near_core = swap(kv_near, "core")
    queries = spread(query_states, "y", 4)
    first, second = (
        jnp.where(z_hi == 0, out_grad, other_grad),
        jnp.where(z_hi == 0, other_grad, out_grad),
    )
    all_grad = spread(jnp.concatenate([first, second], axis=1), "x", 4)
    kv_far_core = swap(kv_far, "core")
    keys_values = (kv_near, kv_far, kv_near_core, kv_far_core)
    grad_attn = jnp.einsum(
        "xrd,xdc->rc",
        all_grad,
        out_weight.reshape(4, 1024, WIDE),
        preferred_element_type=jnp.float32,
    ).astype(jnp.bfloat16)

    (partial_out,) = call(
        forward_kernel,
        [(4, ROWS + EXTRA, WIDE)],
        [pltpu.VMEM((2048, WIDE), jnp.float32), pltpu.VMEM((HD, 2048), jnp.bfloat16)],
        smem,
        (queries,) + keys_values,
        1 << 30,
    )
    parts = lax.all_to_all(partial_out, "y", 0, 0)
    attn_out, send = call(
        combine_kernel,
        [(ROWS, WIDE), (4, ROWS + EXTRA, WIDE)],
        [],
        (),
        (parts, grad_attn),
        1 << 20,
    )
    grads = lax.all_to_all(send, "y", 0, 0)
    terms = jnp.einsum(
        "rc,xdc->xrd",
        attn_out,
        out_weight.reshape(4, 1024, WIDE),
        preferred_element_type=jnp.float32,
    ).astype(jnp.bfloat16)
    terms = lax.all_to_all(terms, "x", 0, 0)
    terms = jnp.sum(terms.astype(jnp.float32), axis=0)
    keep = jnp.where(z_hi == 0, terms[:, :512], terms[:, 512:])
    give = jnp.where(z_hi == 0, terms[:, 512:], terms[:, :512]).astype(jnp.bfloat16)
    got = swap(give, "z_hi")
    projected = (keep + got.astype(jnp.float32)).astype(jnp.bfloat16)

    dq, own, far = call(
        backward_kernel,
        [(4, ROWS, WIDE), (4, 2, ROWS, WIDE), (4, 2, ROWS, WIDE)],
        [
            pltpu.VMEM((2048, HD), jnp.float32),
            pltpu.VMEM((2048, HD), jnp.float32),
            pltpu.VMEM((HD, 2048), jnp.bfloat16),
        ],
        smem,
        (queries, grads) + keys_values,
        1 << 31,
    )
    far = swap(far, "core")
    both = (own.astype(jnp.float32) + far.astype(jnp.float32)).astype(jnp.bfloat16)
    both = jnp.sum(lax.all_to_all(both, "z10", 0, 0).astype(jnp.float32), axis=0)
    late = swap(both[1].astype(jnp.bfloat16), "z2")
    dq = jnp.sum(lax.all_to_all(dq, "y", 0, 0).astype(jnp.float32), axis=0)
    grad_query = dq.astype(jnp.bfloat16)
    grad_kv = (both[0] + late.astype(jnp.float32)).astype(jnp.bfloat16)
    return projected, grad_query, grad_kv[:, :HD], grad_kv[:, HD:]


def solution(mesh):
    fine = Mesh(
        mesh.devices.reshape(2, 4, 4, 2, 4, 2), ("z2", "z10", "y", "core", "x", "z_hi")
    )
    ctx, head = ("z2", "z10", "y", "core"), ("x", "z_hi")
    both = P(ctx, head)
    return jax.shard_map(
        per_device,
        mesh=fine,
        in_specs=(both, both, both, P(None, head), both, P(), P()),
        out_specs=(both, both, both, both),
        check_vma=False,
    )
```

```python
import functools
import math

import jax
import jax.numpy as jnp
from jax import lax
from jax.experimental import pallas as pl
from jax.experimental.pallas import tpu as pltpu
from jax.sharding import Mesh
from jax.sharding import PartitionSpec as P

HD = 128
BLOCK = 64
ROWS = 128
WIDE = 2 * HD
EXTRA = 32
CHUNK = 256
CHUNKS = 8
DOCS = 16
NEGATIVE = -1e30
SCALE = HD ** (-0.5)
SCALE2 = SCALE * math.log2(math.e)
VMEM = 40 * 1024 * 1024

NT = (((1,), (1,)), ((), ()))
NN = (((1,), (0,)), ((), ()))


def mm(a, b, dims):
    return lax.dot_general(a, b, dims, preferred_element_type=jnp.float32)


def heads_down(x):
    return jnp.concatenate([x[:, :HD], x[:, HD:]], axis=0)


def heads_across(x):
    return jnp.concatenate([x[:ROWS], x[ROWS:]], axis=1)


def split3(x):
    hi = x.astype(jnp.bfloat16)
    rest = x - hi.astype(jnp.float32)
    mid = rest.astype(jnp.bfloat16)
    low = (rest - mid.astype(jnp.float32)).astype(jnp.bfloat16)
    return hi, mid, low


def join3(rows, at):
    return rows[at : at + 1] + rows[at + 1 : at + 2] + rows[at + 2 : at + 3]


def query_rows(at_ref, order_ref, lengths_ref, t):
    z_lo, core = at_ref[0], at_ref[2]
    ctx = (z_lo * 4 + t) * 2 + core
    lane = lax.broadcasted_iota(jnp.int32, (1, WIDE), 1)
    row = lax.rem(lane, ROWS)
    first, second = order_ref[2 * ctx] * BLOCK, order_ref[2 * ctx + 1] * BLOCK
    pos = jnp.where(row < BLOCK, first + row, second + row - BLOCK)
    start = jnp.zeros_like(pos)
    end = 0
    for d in range(DOCS):
        end = end + lengths_ref[d]
        start = jnp.where(pos >= end, end, start)
    return pos, start


def key_base(at_ref, order_ref, block):
    z_lo, y, core = at_ref[0], at_ref[1], at_ref[2]
    half, flips = block % 2, (block // 2) % 4 * 2
    flips = (flips & 2) * 2 + (flips & 4) // 2 + (block // 8) % 2
    z_lo = jnp.bitwise_xor(z_lo, flips)
    core = (1 - core) if block // 16 else core
    ctx = (z_lo * 4 + y) * 2 + core
    return order_ref[2 * ctx + half] * BLOCK


def allowed(pos, start, base):
    row = lax.broadcasted_iota(jnp.int32, (BLOCK, WIDE), 0)
    return (row >= start - base) & (row <= pos - base)


def kv_chunk(kv_refs, c, which):
    ref = kv_refs[c // 2]
    first = 2 * (c % 2)
    columns = slice(which * HD, (which + 1) * HD)
    return jnp.concatenate([ref[first, :, columns], ref[first + 1, :, columns]], axis=0)


def forward_kernel(
    at_ref, order_ref, lengths_ref, q_ref, kv0, kv1, kv2, kv3, out_ref, sums_ref, scores, v_t
):
    kv_refs = (kv0, kv1, kv2, kv3)
    for c in range(CHUNKS):
        v_t[:, c * CHUNK : (c + 1) * CHUNK] = kv_chunk(kv_refs, c, 1).T

    def tile(t, carried):
        queries = heads_down(q_ref[t])
        pos, start = query_rows(at_ref, order_ref, lengths_ref, t)
        top = jnp.full((1, WIDE), NEGATIVE, jnp.float32)
        for c in range(CHUNKS):
            s = mm(kv_chunk(kv_refs, c, 0), queries, NT)
            for b in range(CHUNK // BLOCK):
                base = key_base(at_ref, order_ref, c * 4 + b)
                part = jnp.where(
                    allowed(pos, start, base), s[b * BLOCK : (b + 1) * BLOCK], NEGATIVE
                )
                scores[pl.ds(c * CHUNK + b * BLOCK, BLOCK), :] = part
                top = jnp.maximum(top, jnp.max(part, axis=0, keepdims=True))
        top = jnp.maximum(top, 0.1 * NEGATIVE)
        total = jnp.zeros((1, WIDE), jnp.float32)
        acc = jnp.zeros((HD, WIDE), jnp.float32)
        for c in range(CHUNKS):
            e = jnp.exp2((scores[pl.ds(c * CHUNK, CHUNK), :] - top) * SCALE2)
            total = total + jnp.sum(e, axis=0, keepdims=True)
            acc = acc + mm(v_t[:, c * CHUNK : (c + 1) * CHUNK], e.astype(jnp.bfloat16), NN)
        some = total > 0
        safe = jnp.where(some, total, 1.0)
        out_ref[t] = heads_across((acc * (1.0 / safe)).T).astype(jnp.bfloat16)
        sums_ref[t] = jnp.where(some, top * SCALE2 + jnp.log2(safe), NEGATIVE)
        return carried

    lax.fori_loop(0, 4, tile, 0)


def pack_kernel(out_ref, sums_ref, grad_ref, send_ref):
    rows = []
    for t in range(4):
        dots = []
        for h in range(2):
            lanes = slice(h * HD, (h + 1) * HD)
            product = out_ref[t, :, lanes].astype(jnp.float32) * grad_ref[
                t, :, lanes
            ].astype(jnp.float32)
            dot = jnp.sum(product, axis=1, keepdims=True)
            dots.append(jnp.broadcast_to(dot, (ROWS, HD)).T[0:1])
        pieces = split3(sums_ref[t]) + split3(jnp.concatenate(dots, axis=1))
        rows += [v.astype(jnp.float32) for v in pieces]
        rows.append(jnp.zeros((2, WIDE), jnp.float32))
    extra = jnp.concatenate(rows, axis=0).astype(jnp.bfloat16)
    for t in range(4):
        send_ref[t, :ROWS, :] = out_ref[t]
        send_ref[t, ROWS:, :] = extra


def joined(log_sums):
    top = functools.reduce(jnp.maximum, log_sums)
    weights = [jnp.exp2(s - top) for s in log_sums]
    total = functools.reduce(jnp.add, weights)
    inverse = 1.0 / total
    return top + jnp.log2(total), [w * inverse for w in weights]


def combine_kernel(at_ref, parts_ref, weight_ref, terms_ref, sums):
    for j in range(4):
        extra = parts_ref[j, ROWS:, :].astype(jnp.float32)
        for t in range(4):
            sums[t, j : j + 1, :] = join3(extra, 8 * t)
    mine = sums[at_ref[1]]
    log_sum, weights = joined([mine[j : j + 1] for j in range(4)])
    flat = []
    for w in weights:
        flat += [w[:, :HD], w[:, HD:]]
    columns = jnp.concatenate(flat + [jnp.zeros((HD - 8, HD), jnp.float32)], axis=0).T
    halves = []
    for h in range(2):
        lanes = slice(h * HD, (h + 1) * HD)
        acc = jnp.zeros((ROWS, HD), jnp.float32)
        for j in range(4):
            acc = acc + columns[:, 2 * j + h : 2 * j + h + 1] * parts_ref[
                j, :ROWS, lanes
            ].astype(jnp.float32)
        halves.append(acc.astype(jnp.bfloat16))
    attn_out = jnp.concatenate(halves, axis=1)
    for x in range(4):
        for c in range(4):
            part = mm(attn_out, weight_ref[x, pl.ds(c * WIDE, WIDE), :], NT)
            terms_ref[x, :, c * WIDE : (c + 1) * WIDE] = part.astype(jnp.bfloat16)


def backward_kernel(
    at_ref,
    order_ref,
    lengths_ref,
    q_ref,
    grad_ref,
    parts_ref,
    terms_ref,
    kv0,
    kv1,
    kv2,
    kv3,
    dq_ref,
    own_ref,
    far_ref,
    dk_acc,
    dv_acc,
    k_t,
    stats,
):
    kv_refs = (kv0, kv1, kv2, kv3)
    for c in range(CHUNKS):
        k_t[:, c * CHUNK : (c + 1) * CHUNK] = kv_chunk(kv_refs, c, 0).T
    dk_acc[...] = jnp.zeros_like(dk_acc)
    dv_acc[...] = jnp.zeros_like(dv_acc)
    extras = [parts_ref[j, ROWS:, :].astype(jnp.float32) for j in range(4)]
    for t in range(4):
        log_sum, weights = joined([join3(e, 8 * t) for e in extras])
        dots = [w * join3(e, 8 * t + 3) for w, e in zip(weights, extras)]
        stats[t, 0:1, :] = log_sum
        stats[t, 1:2, :] = functools.reduce(jnp.add, dots)

    def tile(t, carried):
        queries = heads_down(q_ref[t])
        grads = heads_down(grad_ref[t])
        log_sum, row_dots = stats[t, 0:1, :], stats[t, 1:2, :]
        pos, start = query_rows(at_ref, order_ref, lengths_ref, t)
        dq = jnp.zeros((HD, WIDE), jnp.float32)
        for c in range(CHUNKS):
            rows = pl.ds(c * CHUNK, CHUNK)
            s = mm(kv_chunk(kv_refs, c, 0), queries, NT)
            dp = mm(kv_chunk(kv_refs, c, 1), grads, NT)
            parts = []
            for b in range(CHUNK // BLOCK):
                base = key_base(at_ref, order_ref, c * 4 + b)
                raised = jnp.exp2(s[b * BLOCK : (b + 1) * BLOCK] * SCALE2 - log_sum)
                parts.append(jnp.where(allowed(pos, start, base), raised, 0.0))
            p = jnp.concatenate(parts, axis=0)
            ds = (p * (dp - row_dots)).astype(jnp.bfloat16)
            dv_acc[rows, :] += mm(p.astype(jnp.bfloat16), grads, NN)
            dk_acc[rows, :] += mm(ds, queries, NN)
            dq = dq + mm(k_t[:, c * CHUNK : (c + 1) * CHUNK], ds, NN)
        dq_ref[t] = heads_across((dq * SCALE).T).astype(jnp.bfloat16)
        return carried

    lax.fori_loop(0, 4, tile, 0)
    for part in range(4):
        ref = far_ref if part // 2 else own_ref
        for k in range(4):
            rows = pl.ds((part * 4 + k) * ROWS, ROWS)
            z10 = jnp.bitwise_xor(at_ref[0] % 4, (k // 2) * 2 + part % 2)
            ref[z10, k % 2, :, :HD] = (dk_acc[rows, :] * SCALE).astype(jnp.bfloat16)
            ref[z10, k % 2, :, HD:] = dv_acc[rows, :].astype(jnp.bfloat16)


def call(kernel, outs, scratch, smem, vmem, flops, unread=0):
    specs = [pl.BlockSpec(memory_space=pltpu.SMEM)] * len(smem)
    specs += [pl.BlockSpec(memory_space=pltpu.VMEM)] * len(vmem)
    if unread:
        specs[unread] = pl.BlockSpec(memory_space=pl.ANY)
    out_specs = [pl.BlockSpec(memory_space=pltpu.VMEM)] * len(outs)
    return pl.pallas_call(
        kernel,
        out_shape=[jax.ShapeDtypeStruct(*o) for o in outs],
        in_specs=specs,
        out_specs=out_specs,
        scratch_shapes=scratch,
        compiler_params=pltpu.CompilerParams(vmem_limit_bytes=VMEM),
        cost_estimate=pl.CostEstimate(flops=flops, bytes_accessed=1 << 21, transcendentals=1 << 21),
    )(*smem, *vmem)


def spread(x, axis, n):
    return lax.all_to_all(jnp.broadcast_to(x, (n,) + x.shape), axis, 0, 0)


def swap(x, axis):
    return lax.ppermute(x, axis, [(0, 1), (1, 0)])


def per_device(
    query_states, key_states, value_states, out_weight, out_grad, doc_lengths, block_order
):
    z_hi = lax.axis_index("z_hi")
    z_lo = lax.axis_index("z2") * 4 + lax.axis_index("z1") * 2 + lax.axis_index("z0")
    at = jnp.stack([z_lo, lax.axis_index("y"), lax.axis_index("core")]).astype(jnp.int32)
    smem = (at, block_order, doc_lengths)

    other_grad = swap(out_grad, "z_hi")
    kv = jnp.concatenate([key_states, value_states], axis=1)
    kv = jnp.stack([kv, swap(kv, "z2")])
    queries = spread(query_states, "y", 4)
    out_grad, other_grad, kv, queries = lax.optimization_barrier(
        (out_grad, other_grad, kv, queries)
    )
    first, second = (
        jnp.where(z_hi == 0, out_grad, other_grad),
        jnp.where(z_hi == 0, other_grad, out_grad),
    )
    all_grad = spread(jnp.concatenate([first, second], axis=1), "x", 4)
    kv_near = jnp.concatenate([kv, swap(kv, "z1")], axis=0)
    kv_far = swap(kv_near, "z0")
    kv_near_core = swap(kv_near, "core")
    kv_far_core = swap(kv_far, "core")
    keys_values = (kv_near, kv_far, kv_near_core, kv_far_core)
    weight = out_weight.reshape(4, 1024, WIDE)
    grad_attn = jnp.einsum(
        "xrd,xdc->rc", all_grad, weight, preferred_element_type=jnp.float32
    ).astype(jnp.bfloat16)
    grads = spread(grad_attn, "y", 4)

    bf16, f32 = jnp.bfloat16, jnp.float32
    partial_out, partial_sums = call(
        forward_kernel,
        [((4, ROWS, WIDE), bf16), ((4, 1, WIDE), f32)],
        [pltpu.VMEM((2048, WIDE), f32), pltpu.VMEM((HD, 2048), bf16)],
        smem,
        (queries,) + keys_values,
        8 * 10**9,
    )
    (send,) = call(
        pack_kernel,
        [((4, ROWS + EXTRA, WIDE), bf16)],
        [],
        (),
        (partial_out, partial_sums, grads),
        10**9,
    )
    parts = lax.all_to_all(send, "y", 0, 0)
    (terms,) = call(
        combine_kernel,
        [((4, ROWS, 1024), bf16)],
        [pltpu.VMEM((4, 8, WIDE), f32)],
        (at,),
        (parts, weight),
        10**9,
    )
    all_terms = lax.all_to_all(terms, "x", 0, 0)
    dq, own, far = call(
        backward_kernel,
        [((4, ROWS, WIDE), bf16), ((4, 2, ROWS, WIDE), bf16), ((4, 2, ROWS, WIDE), bf16)],
        [
            pltpu.VMEM((2048, HD), f32),
            pltpu.VMEM((2048, HD), f32),
            pltpu.VMEM((HD, 2048), bf16),
            pltpu.VMEM((4, 8, WIDE), f32),
        ],
        smem,
        (queries, grads, parts, terms) + keys_values,
        12 * 10**9,
        unread=6,
    )
    dq, own, far, all_terms = lax.optimization_barrier((dq, own, far, all_terms))
    all_terms = jnp.sum(all_terms.astype(f32), axis=0)
    keep = jnp.where(z_hi == 0, all_terms[:, :512], all_terms[:, 512:])
    give = jnp.where(z_hi == 0, all_terms[:, 512:], all_terms[:, :512]).astype(bf16)
    got = swap(give, "z_hi")
    projected = (keep + got.astype(f32)).astype(bf16)
    far = swap(far, "core")
    both = (own.astype(f32) + far.astype(f32)).astype(bf16)
    both = lax.all_to_all(both, ("z1", "z0"), 0, 0)
    both, dq = lax.optimization_barrier((both, dq))
    both = jnp.sum(both.astype(f32), axis=0)
    late = swap(both[1].astype(bf16), "z2")
    grad_kv = (both[0] + late.astype(f32)).astype(bf16)
    dq = jnp.sum(lax.all_to_all(dq, "y", 0, 0).astype(f32), axis=0)
    grad_query = dq.astype(bf16)
    return projected, grad_query, grad_kv[:, :HD], grad_kv[:, HD:]


def solution(mesh):
    fine = Mesh(
        mesh.devices.reshape(2, 2, 2, 4, 2, 4, 2),
        ("z2", "z1", "z0", "y", "core", "x", "z_hi"),
    )
    ctx, head = ("z2", "z1", "z0", "y", "core"), ("x", "z_hi")
    both = P(ctx, head)
    return jax.shard_map(
        per_device,
        mesh=fine,
        in_specs=(both, both, both, P(None, head), both, P(), P()),
        out_specs=(both, both, both, both),
        check_vma=False,
    )
```

```python
import functools
import math

import jax
import jax.numpy as jnp
from jax import lax
from jax.experimental import pallas as pl
from jax.experimental.pallas import tpu as pltpu
from jax.sharding import Mesh
from jax.sharding import PartitionSpec as P

HD = 128
BLOCK = 64
ROWS = 128
WIDE = 2 * HD
EXTRA = 32
CHUNK = 256
CHUNKS = 8
DOCS = 16
NEGATIVE = -1e30
SCALE = HD ** (-0.5)
SCALE2 = SCALE * math.log2(math.e)
VMEM = 20 * 1024 * 1024

NT = (((1,), (1,)), ((), ()))
NN = (((1,), (0,)), ((), ()))


def mm(a, b, dims):
    return lax.dot_general(a, b, dims, preferred_element_type=jnp.float32)


def heads_down(x):
    return jnp.concatenate([x[:, :HD], x[:, HD:]], axis=0)


def heads_across(x):
    return jnp.concatenate([x[:ROWS], x[ROWS:]], axis=1)


def split3(x):
    hi = x.astype(jnp.bfloat16)
    rest = x - hi.astype(jnp.float32)
    mid = rest.astype(jnp.bfloat16)
    low = (rest - mid.astype(jnp.float32)).astype(jnp.bfloat16)
    return hi, mid, low


def join3(rows, at):
    return rows[at : at + 1] + rows[at + 1 : at + 2] + rows[at + 2 : at + 3]


K_RANK, K_BASE, Q_ORDER, Q_BASE, Q_RANK, Q_LOW, Q_RAW = 0, 32, 64, 72, 80, 88, 96


def key_base(at_ref, order_ref, block):
    half, k = block % 2, (block // 2) % 8
    z_lo = (k % 2) * 4 + (k // 2 % 2) * 2 + k // 4
    core = (1 - at_ref[2]) if block // 16 else at_ref[2]
    ctx = (z_lo * 4 + at_ref[1]) * 2 + core
    return order_ref[2 * ctx + half] * BLOCK


def plan_kernel(at_ref, order_ref, lengths_ref, plan_ref, raw):
    def rank(values, count, at, base_at):
        def one(b, carried):
            mine, place = values[b], 0
            for j in range(count):
                place = place + jnp.where(values[j] < mine, 1, 0)
            plan_ref[at + b] = place
            plan_ref[base_at + place] = mine
            return carried

        lax.fori_loop(0, count, one, 0)

    for b in range(32):
        raw[b] = key_base(at_ref, order_ref, b)
    rank(raw, 32, K_RANK, K_BASE)
    for b in range(8):
        ctx = (at_ref[0] * 4 + b // 2) * 2 + at_ref[2]
        raw[b] = order_ref[2 * ctx + b % 2] * BLOCK
    rank(raw, 8, Q_RANK, Q_BASE)
    for b in range(8):
        plan_ref[Q_ORDER + plan_ref[Q_RANK + b]] = b
    for b in range(8):
        first, low, end = plan_ref[Q_BASE + b], 0, 0
        for d in range(DOCS):
            end = end + lengths_ref[d]
            low = jnp.where(first >= end, end, low)
        plan_ref[Q_LOW + b] = low


def query_rows(plan_ref, lengths_ref, t):
    lane = lax.broadcasted_iota(jnp.int32, (1, WIDE), 1)
    row = lax.rem(lane, ROWS)
    first, second = plan_ref[Q_BASE + 2 * t], plan_ref[Q_BASE + 2 * t + 1]
    pos = jnp.where(row < BLOCK, first + row, second + row - BLOCK)
    start = jnp.zeros_like(pos)
    end = 0
    for d in range(DOCS):
        end = end + lengths_ref[d]
        start = jnp.where(pos >= end, end, start)
    return pos, start


def reached(plan_ref, t, c):
    low, high = plan_ref[K_BASE + 4 * c], plan_ref[K_BASE + 4 * c + 3] + BLOCK - 1
    seen = []
    for i in range(2):
        at = 2 * t + i
        last = plan_ref[Q_BASE + at] + BLOCK - 1
        seen.append((low <= last) & (high >= plan_ref[Q_LOW + at]))
    return seen[0] | seen[1]


def allowed(pos, start, base):
    row = lax.broadcasted_iota(jnp.int32, (BLOCK, WIDE), 0)
    return (row >= start - base) & (row <= pos - base)


def sort_keys(plan_ref, kv_refs, k_s, v_s):
    for b in range(32):
        rows = pl.ds(pl.multiple_of(plan_ref[K_RANK + b] * BLOCK, BLOCK), BLOCK)
        ref = kv_refs[b // 16]
        half = pl.ds((b % 2) * BLOCK, BLOCK)
        k_s[rows, :] = ref[b % 16 // 2, half, :HD]
        v_s[rows, :] = ref[b % 16 // 2, half, HD:]


def two_blocks(ref, plan_ref, t):
    first, second = ref[plan_ref[Q_ORDER + 2 * t]], ref[plan_ref[Q_ORDER + 2 * t + 1]]
    return jnp.concatenate([first[:, :HD], second[:, :HD], first[:, HD:], second[:, HD:]], axis=0)


def forward_kernel(
    plan_ref, lengths_ref, q_ref, kv0, kv1, out_ref, sums_ref, scores, k_s, v_s, v_t, top, total, acc
):
    sort_keys(plan_ref, (kv0, kv1), k_s, v_s)
    for c in range(CHUNKS):
        v_t[:, c * CHUNK : (c + 1) * CHUNK] = v_s[c * CHUNK : (c + 1) * CHUNK, :].T

    def tile(t, carried):
        queries = two_blocks(q_ref, plan_ref, t)
        pos, start = query_rows(plan_ref, lengths_ref, t)
        top[...] = jnp.full((1, WIDE), 0.1 * NEGATIVE, jnp.float32)
        total[...] = jnp.zeros((1, WIDE), jnp.float32)
        acc[...] = jnp.zeros((HD, WIDE), jnp.float32)
        for c in range(CHUNKS):

            @pl.when(reached(plan_ref, t, c))
            def _():
                s = mm(k_s[c * CHUNK : (c + 1) * CHUNK, :], queries, NT)
                most = top[...]
                for b in range(CHUNK // BLOCK):
                    base = plan_ref[K_BASE + c * 4 + b]
                    part = jnp.where(
                        allowed(pos, start, base), s[b * BLOCK : (b + 1) * BLOCK], NEGATIVE
                    )
                    scores[pl.ds(c * CHUNK + b * BLOCK, BLOCK), :] = part
                    most = jnp.maximum(most, jnp.max(part, axis=0, keepdims=True))
                top[...] = most

        for c in range(CHUNKS):

            @pl.when(reached(plan_ref, t, c))
            def _():
                e = jnp.exp2((scores[pl.ds(c * CHUNK, CHUNK), :] - top[...]) * SCALE2)
                total[...] += jnp.sum(e, axis=0, keepdims=True)
                acc[...] += mm(v_t[:, c * CHUNK : (c + 1) * CHUNK], e.astype(jnp.bfloat16), NN)

        some = total[...] > 0
        safe = jnp.where(some, total[...], 1.0)
        out = heads_across((acc[...] * (1.0 / safe)).T).astype(jnp.bfloat16)
        out_ref[plan_ref[Q_ORDER + 2 * t]] = out[:BLOCK]
        out_ref[plan_ref[Q_ORDER + 2 * t + 1]] = out[BLOCK:]
        sums_ref[t] = jnp.where(some, top[...] * SCALE2 + jnp.log2(safe), NEGATIVE)
        return carried

    lax.fori_loop(0, 4, tile, 0)


def both_kernel(at_ref, own_ref, other_ref, send_ref):
    mine = at_ref[3]
    for j in range(4):
        send_ref[j, mine] = own_ref[...]
        send_ref[j, 1 - mine] = other_ref[...]


def grad_kernel(all_ref, weight_ref, send_ref):
    acc = jnp.zeros((ROWS, WIDE), jnp.float32)
    for x in range(4):
        for z in range(2):
            acc = acc + mm(all_ref[x, z], weight_ref[x, z], NN)
    for j in range(4):
        send_ref[j] = acc.astype(jnp.bfloat16)


def pack_kernel(plan_ref, out_ref, sums_ref, grad_ref, send_ref):
    rows = []
    for t in range(4):
        dots = []
        for h in range(2):
            lanes = slice(h * HD, (h + 1) * HD)
            halves = []
            for i in range(2):
                at = plan_ref[Q_ORDER + 2 * t + i]
                product = out_ref[at][:, lanes].astype(jnp.float32) * grad_ref[at][
                    :, lanes
                ].astype(jnp.float32)
                halves.append(jnp.sum(product, axis=1, keepdims=True))
            dot = jnp.concatenate(halves, axis=0)
            dots.append(jnp.broadcast_to(dot, (ROWS, HD)).T[0:1])
        pieces = split3(sums_ref[t]) + split3(jnp.concatenate(dots, axis=1))
        rows += [v.astype(jnp.float32) for v in pieces]
        rows.append(jnp.zeros((2, WIDE), jnp.float32))
    extra = jnp.concatenate(rows, axis=0).astype(jnp.bfloat16)
    for t in range(4):
        send_ref[t, :BLOCK, :] = out_ref[2 * t]
        send_ref[t, BLOCK:ROWS, :] = out_ref[2 * t + 1]
        send_ref[t, ROWS:, :] = extra


def joined(log_sums):
    top = functools.reduce(jnp.maximum, log_sums)
    weights = [jnp.exp2(s - top) for s in log_sums]
    total = functools.reduce(jnp.add, weights)
    inverse = 1.0 / total
    return top + jnp.log2(total), [w * inverse for w in weights]


def combine_kernel(at_ref, plan_ref, parts_ref, weight_ref, terms_ref, sums):
    for j in range(4):
        extra = parts_ref[j, ROWS:, :].astype(jnp.float32)
        for t in range(4):
            sums[t, j : j + 1, :] = join3(extra, 8 * t)
    lane = lax.rem(lax.broadcasted_iota(jnp.int32, (8, WIDE), 1), ROWS)
    first, second = plan_ref[Q_RANK + 2 * at_ref[1]], plan_ref[Q_RANK + 2 * at_ref[1] + 1]
    low, high = sums[first // 2], sums[second // 2]
    low = jnp.where(first % 2 == 1, pltpu.roll(low, WIDE - BLOCK, 1), low)
    high = jnp.where(second % 2 == 0, pltpu.roll(high, BLOCK, 1), high)
    mine = jnp.where(lane < BLOCK, low, high)
    log_sum, weights = joined([mine[j : j + 1] for j in range(4)])
    flat = []
    for w in weights:
        flat += [w[:, :HD], w[:, HD:]]
    columns = jnp.concatenate(flat + [jnp.zeros((HD - 8, HD), jnp.float32)], axis=0).T
    halves = []
    for h in range(2):
        lanes = slice(h * HD, (h + 1) * HD)
        acc = jnp.zeros((ROWS, HD), jnp.float32)
        for j in range(4):
            acc = acc + columns[:, 2 * j + h : 2 * j + h + 1] * parts_ref[
                j, :ROWS, lanes
            ].astype(jnp.float32)
        halves.append(acc.astype(jnp.bfloat16))
    attn_out = jnp.concatenate(halves, axis=1)
    for x in range(4):
        for c in range(4):
            part = mm(attn_out, weight_ref[x, pl.ds(c * WIDE, WIDE), :], NT)
            terms_ref[x, :, c * WIDE : (c + 1) * WIDE] = part.astype(jnp.bfloat16)


def backward_kernel(
    at_ref,
    plan_ref,
    lengths_ref,
    q_ref,
    grad_ref,
    parts_ref,
    terms_ref,
    kv0,
    kv1,
    dq0_ref,
    dq1_ref,
    dq2_ref,
    dq3_ref,
    own_ref,
    far_ref,
    dk_acc,
    dv_acc,
    k_s,
    v_s,
    k_t,
    stats,
    dq_parts,
    dq_acc,
):
    sort_keys(plan_ref, (kv0, kv1), k_s, v_s)
    for c in range(CHUNKS):
        k_t[:, c * CHUNK : (c + 1) * CHUNK] = k_s[c * CHUNK : (c + 1) * CHUNK, :].T
    dk_acc[...] = jnp.zeros_like(dk_acc)
    dv_acc[...] = jnp.zeros_like(dv_acc)
    extras = [parts_ref[j, ROWS:, :].astype(jnp.float32) for j in range(4)]
    for t in range(4):
        log_sum, weights = joined([join3(e, 8 * t) for e in extras])
        dots = [w * join3(e, 8 * t + 3) for w, e in zip(weights, extras)]
        stats[t, 0:1, :] = log_sum
        stats[t, 1:2, :] = functools.reduce(jnp.add, dots)

    def tile(t, carried):
        queries = two_blocks(q_ref, plan_ref, t)
        grads = two_blocks(grad_ref, plan_ref, t)
        log_sum, row_dots = stats[t, 0:1, :], stats[t, 1:2, :]
        pos, start = query_rows(plan_ref, lengths_ref, t)
        dq_acc[...] = jnp.zeros((HD, WIDE), jnp.float32)
        for c in range(CHUNKS):

            @pl.when(reached(plan_ref, t, c))
            def _():
                rows = pl.ds(c * CHUNK, CHUNK)
                s = mm(k_s[rows, :], queries, NT)
                dp = mm(v_s[rows, :], grads, NT)
                parts = []
                for b in range(CHUNK // BLOCK):
                    base = plan_ref[K_BASE + c * 4 + b]
                    raised = jnp.exp2(s[b * BLOCK : (b + 1) * BLOCK] * SCALE2 - log_sum)
                    parts.append(jnp.where(allowed(pos, start, base), raised, 0.0))
                p = jnp.concatenate(parts, axis=0)
                ds = (p * (dp - row_dots)).astype(jnp.bfloat16)
                dv_acc[rows, :] += mm(p.astype(jnp.bfloat16), grads, NN)
                dk_acc[rows, :] += mm(ds, queries, NN)
                dq_acc[...] += mm(k_t[:, c * CHUNK : (c + 1) * CHUNK], ds, NN)

        dq = heads_across((dq_acc[...] * SCALE).T).astype(jnp.bfloat16)
        for i in range(2):
            at = plan_ref[Q_ORDER + 2 * t + i]
            slot = jnp.bitwise_xor(at // 2, at_ref[1]) * 2 + at % 2
            dq_parts[slot] = dq[i * BLOCK : (i + 1) * BLOCK]
        return carried

    lax.fori_loop(0, 4, tile, 0)
    for k, ref in enumerate((dq0_ref, dq1_ref, dq2_ref, dq3_ref)):
        ref[:BLOCK, :] = dq_parts[2 * k]
        ref[BLOCK:, :] = dq_parts[2 * k + 1]
    z2 = at_ref[0] // 4
    for b in range(32):
        ref = far_ref if b // 16 else own_ref
        k = b % 16 // 2
        rows = pl.ds(pl.multiple_of(plan_ref[K_RANK + b] * BLOCK, BLOCK), BLOCK)
        half = pl.ds((b % 2) * BLOCK, BLOCK)
        z10 = (k // 2 % 2) * 2 + k // 4
        z2_flip = jnp.bitwise_xor(z2, k % 2)
        ref[z10, z2_flip, half, :HD] = (dk_acc[rows, :] * SCALE).astype(jnp.bfloat16)
        ref[z10, z2_flip, half, HD:] = dv_acc[rows, :].astype(jnp.bfloat16)


def call(kernel, outs, scratch, smem, vmem, flops, unread=0, space=pltpu.VMEM):
    specs = [pl.BlockSpec(memory_space=pltpu.SMEM)] * len(smem)
    specs += [pl.BlockSpec(memory_space=pltpu.VMEM)] * len(vmem)
    if unread:
        specs[unread] = pl.BlockSpec(memory_space=pl.ANY)
    out_specs = [pl.BlockSpec(memory_space=space)] * len(outs)
    return pl.pallas_call(
        kernel,
        out_shape=[jax.ShapeDtypeStruct(*o) for o in outs],
        in_specs=specs,
        out_specs=out_specs,
        scratch_shapes=scratch,
        compiler_params=pltpu.CompilerParams(vmem_limit_bytes=VMEM),
        cost_estimate=pl.CostEstimate(flops=flops, bytes_accessed=1 << 21, transcendentals=1 << 21),
    )(*smem, *vmem)


def spread(x, axis, n):
    return lax.all_to_all(jnp.broadcast_to(x, (n,) + x.shape), axis, 0, 0)


def gather(x, axis):
    return lax.all_gather(x, axis, axis=0)


def swap(x, axis):
    return lax.ppermute(x, axis, [(0, 1), (1, 0)])


def per_device(
    query_states, key_states, value_states, out_weight, out_grad, doc_lengths, block_order
):
    z_hi = lax.axis_index("z_hi")
    z_lo = lax.axis_index("z2") * 4 + lax.axis_index("z1") * 2 + lax.axis_index("z0")
    at = jnp.stack([z_lo, lax.axis_index("y"), lax.axis_index("core"), z_hi]).astype(jnp.int32)
    smem = (at, block_order, doc_lengths)

    bf16, f32 = jnp.bfloat16, jnp.float32
    other_grad = swap(out_grad, "z_hi")
    queries = spread(query_states, "y", 4)
    kv = jnp.concatenate([key_states, value_states], axis=1)
    (plan,) = call(
        plan_kernel,
        [((ROWS,), jnp.int32)],
        [pltpu.SMEM((32,), jnp.int32)],
        smem,
        (),
        10**8,
        space=pltpu.SMEM,
    )
    out_grad, other_grad, kv, queries, plan = lax.optimization_barrier(
        (out_grad, other_grad, kv, queries, plan)
    )
    queries = queries.reshape(8, BLOCK, WIDE)
    lookup = (plan, doc_lengths)
    (send,) = call(
        both_kernel, [((4, 2, ROWS, 512), bf16)], [], (at,), (out_grad, other_grad), 10**8
    )
    send, kv = lax.optimization_barrier((send, kv))
    all_grad = lax.all_to_all(send, "x", 0, 0)
    kv = gather(gather(kv, "z2"), "z1")
    all_grad, kv = lax.optimization_barrier((all_grad, kv))
    (send,) = call(
        grad_kernel,
        [((4, ROWS, WIDE), bf16)],
        [],
        (),
        (all_grad, out_weight.reshape(4, 2, 512, WIDE)),
        10**9,
    )
    send, kv = lax.optimization_barrier((send, kv))
    grads = lax.all_to_all(send, "y", 0, 0).reshape(8, BLOCK, WIDE)
    kv = gather(kv, "z0").reshape(8, ROWS, WIDE)
    keys_values = (kv, swap(kv, "core"))
    weight = out_weight.reshape(4, 1024, WIDE)

    partial_out, partial_sums = call(
        forward_kernel,
        [((8, BLOCK, WIDE), bf16), ((4, 1, WIDE), f32)],
        [
            pltpu.VMEM((2048, WIDE), f32),
            pltpu.VMEM((2048, HD), bf16),
            pltpu.VMEM((2048, HD), bf16),
            pltpu.VMEM((HD, 2048), bf16),
            pltpu.VMEM((1, WIDE), f32),
            pltpu.VMEM((1, WIDE), f32),
            pltpu.VMEM((HD, WIDE), f32),
        ],
        lookup,
        (queries,) + keys_values,
        8 * 10**9,
    )
    (send,) = call(
        pack_kernel,
        [((4, ROWS + EXTRA, WIDE), bf16)],
        [],
        (plan,),
        (partial_out, partial_sums, grads),
        10**9,
    )
    parts = lax.all_to_all(send, "y", 0, 0)
    (terms,) = call(
        combine_kernel,
        [((4, ROWS, 1024), bf16)],
        [pltpu.VMEM((4, 8, WIDE), f32)],
        (at, plan),
        (parts, weight),
        10**9,
    )
    all_terms = lax.all_to_all(terms, "x", 0, 0)
    dq0, dq1, dq2, dq3, own, far = call(
        backward_kernel,
        [((ROWS, WIDE), bf16)] * 4 + [((4, 2, ROWS, WIDE), bf16)] * 2,
        [
            pltpu.VMEM((2048, HD), f32),
            pltpu.VMEM((2048, HD), f32),
            pltpu.VMEM((2048, HD), bf16),
            pltpu.VMEM((2048, HD), bf16),
            pltpu.VMEM((HD, 2048), bf16),
            pltpu.VMEM((4, 8, WIDE), f32),
            pltpu.VMEM((8, BLOCK, WIDE), bf16),
            pltpu.VMEM((HD, WIDE), f32),
        ],
        (at,) + lookup,
        (queries, grads, parts, terms) + keys_values,
        12 * 10**9,
        unread=6,
    )
    own, far, all_terms = lax.optimization_barrier((own, far, all_terms))
    far = swap(far, "core")
    both = (own.astype(f32) + far.astype(f32)).astype(bf16)
    both, dq1, dq2, dq3, all_terms = lax.optimization_barrier(
        (both, dq1, dq2, dq3, all_terms)
    )
    all_terms = jnp.sum(all_terms.astype(f32), axis=0)
    keep = jnp.where(z_hi == 0, all_terms[:, :512], all_terms[:, 512:])
    give = jnp.where(z_hi == 0, all_terms[:, 512:], all_terms[:, :512]).astype(bf16)
    got = swap(give, "z_hi")
    projected = (keep + got.astype(f32)).astype(bf16)
    both = lax.all_to_all(both, ("z1", "z0"), 0, 0)
    partial = [lax.ppermute(x, "y", [(i, i ^ k) for i in range(4)]) for k, x in ((1, dq1), (2, dq2), (3, dq3))]
    dq = dq0.astype(f32)
    for x in partial:
        dq = dq + x.astype(f32)
    grad_query = dq.astype(bf16)
    both = jnp.sum(both.astype(f32), axis=0)
    late = swap(both[1].astype(bf16), "z2")
    grad_kv = (both[0] + late.astype(f32)).astype(bf16)
    return projected, grad_query, grad_kv[:, :HD], grad_kv[:, HD:]


def solution(mesh):
    fine = Mesh(
        mesh.devices.reshape(2, 2, 2, 4, 2, 4, 2),
        ("z2", "z1", "z0", "y", "core", "x", "z_hi"),
    )
    ctx, head = ("z2", "z1", "z0", "y", "core"), ("x", "z_hi")
    both = P(ctx, head)
    return jax.shard_map(
        per_device,
        mesh=fine,
        in_specs=(both, both, both, P(None, head), both, P(), P()),
        out_specs=(both, both, both, both),
        check_vma=False,
    )
```

```python
import functools
import math

import jax
import jax.numpy as jnp
from jax import lax
from jax.experimental import pallas as pl
from jax.experimental.pallas import tpu as pltpu
from jax.sharding import Mesh
from jax.sharding import PartitionSpec as P

HD = 128
BLOCK = 64
ROWS = 128
WIDE = 2 * HD
EXTRA = 32
CHUNK = 256
CHUNKS = 8
DOCS = 16
NEGATIVE = -1e30
SCALE = HD ** (-0.5)
SCALE2 = SCALE * math.log2(math.e)
VMEM = 20 * 1024 * 1024

NT = (((1,), (1,)), ((), ()))
NN = (((1,), (0,)), ((), ()))


def mm(a, b, dims):
    return lax.dot_general(a, b, dims, preferred_element_type=jnp.float32)


def heads_down(x):
    return jnp.concatenate([x[:, :HD], x[:, HD:]], axis=0)


def heads_across(x):
    return jnp.concatenate([x[:ROWS], x[ROWS:]], axis=1)


def split3(x):
    hi = x.astype(jnp.bfloat16)
    rest = x - hi.astype(jnp.float32)
    mid = rest.astype(jnp.bfloat16)
    low = (rest - mid.astype(jnp.float32)).astype(jnp.bfloat16)
    return hi, mid, low


def join3(rows, at):
    return rows[at : at + 1] + rows[at + 1 : at + 2] + rows[at + 2 : at + 3]


K_RANK, K_BASE, Q_ORDER, Q_BASE, Q_RANK, Q_LOW, Q_RAW = 0, 32, 64, 72, 80, 88, 96


def key_base(at_ref, order_ref, block):
    half, k = block % 2, (block // 2) % 8
    z_lo = (k % 2) * 4 + (k // 2 % 2) * 2 + k // 4
    core = (1 - at_ref[2]) if block // 16 else at_ref[2]
    ctx = (z_lo * 4 + at_ref[1]) * 2 + core
    return order_ref[2 * ctx + half] * BLOCK


def plan_kernel(at_ref, order_ref, lengths_ref, plan_ref, raw):
    def rank(values, count, at, base_at):
        def one(b, carried):
            mine, place = values[b], 0
            for j in range(count):
                place = place + jnp.where(values[j] < mine, 1, 0)
            plan_ref[at + b] = place
            plan_ref[base_at + place] = mine
            return carried

        lax.fori_loop(0, count, one, 0)

    for b in range(32):
        raw[b] = key_base(at_ref, order_ref, b)
    rank(raw, 32, K_RANK, K_BASE)
    for b in range(8):
        ctx = (at_ref[0] * 4 + b // 2) * 2 + at_ref[2]
        raw[b] = order_ref[2 * ctx + b % 2] * BLOCK
    rank(raw, 8, Q_RANK, Q_BASE)
    for b in range(8):
        plan_ref[Q_ORDER + plan_ref[Q_RANK + b]] = b
    for b in range(8):
        first, low, end = plan_ref[Q_BASE + b], 0, 0
        for d in range(DOCS):
            end = end + lengths_ref[d]
            low = jnp.where(first >= end, end, low)
        plan_ref[Q_LOW + b] = low


def query_rows(plan_ref, lengths_ref, t):
    lane = lax.broadcasted_iota(jnp.int32, (1, WIDE), 1)
    row = lax.rem(lane, ROWS)
    first, second = plan_ref[Q_BASE + 2 * t], plan_ref[Q_BASE + 2 * t + 1]
    pos = jnp.where(row < BLOCK, first + row, second + row - BLOCK)
    start = jnp.zeros_like(pos)
    end = 0
    for d in range(DOCS):
        end = end + lengths_ref[d]
        start = jnp.where(pos >= end, end, start)
    return pos, start


def reached(plan_ref, t, c):
    low, high = plan_ref[K_BASE + 4 * c], plan_ref[K_BASE + 4 * c + 3] + BLOCK - 1
    seen = []
    for i in range(2):
        at = 2 * t + i
        last = plan_ref[Q_BASE + at] + BLOCK - 1
        seen.append((low <= last) & (high >= plan_ref[Q_LOW + at]))
    return seen[0] | seen[1]


def allowed(pos, start, base):
    row = lax.broadcasted_iota(jnp.int32, (BLOCK, WIDE), 0)
    return (row >= start - base) & (row <= pos - base)


def sort_keys(plan_ref, kv_refs, k_s, v_s):
    for b in range(32):
        rows = pl.ds(pl.multiple_of(plan_ref[K_RANK + b] * BLOCK, BLOCK), BLOCK)
        ref = kv_refs[b // 16]
        half = pl.ds((b % 2) * BLOCK, BLOCK)
        k_s[rows, :] = ref[b % 16 // 2, half, :HD]
        v_s[rows, :] = ref[b % 16 // 2, half, HD:]


def two_blocks(ref, plan_ref, t):
    first, second = ref[plan_ref[Q_ORDER + 2 * t]], ref[plan_ref[Q_ORDER + 2 * t + 1]]
    return jnp.concatenate([first[:, :HD], second[:, :HD], first[:, HD:], second[:, HD:]], axis=0)


def forward_kernel(
    plan_ref, lengths_ref, q_ref, kv0, kv1, out_ref, sums_ref, scores, k_s, v_s, v_t, top, total, acc
):
    sort_keys(plan_ref, (kv0, kv1), k_s, v_s)
    for c in range(CHUNKS):
        v_t[:, c * CHUNK : (c + 1) * CHUNK] = v_s[c * CHUNK : (c + 1) * CHUNK, :].T

    def tile(t, carried):
        queries = two_blocks(q_ref, plan_ref, t)
        pos, start = query_rows(plan_ref, lengths_ref, t)
        top[...] = jnp.full((1, WIDE), 0.1 * NEGATIVE, jnp.float32)
        total[...] = jnp.zeros((1, WIDE), jnp.float32)
        acc[...] = jnp.zeros((HD, WIDE), jnp.float32)
        for c in range(CHUNKS):

            @pl.when(reached(plan_ref, t, c))
            def _():
                s = mm(k_s[c * CHUNK : (c + 1) * CHUNK, :], queries, NT)
                most = top[...]
                for b in range(CHUNK // BLOCK):
                    base = plan_ref[K_BASE + c * 4 + b]
                    part = jnp.where(
                        allowed(pos, start, base), s[b * BLOCK : (b + 1) * BLOCK], NEGATIVE
                    )
                    scores[pl.ds(c * CHUNK + b * BLOCK, BLOCK), :] = part
                    most = jnp.maximum(most, jnp.max(part, axis=0, keepdims=True))
                top[...] = most

        for c in range(CHUNKS):

            @pl.when(reached(plan_ref, t, c))
            def _():
                e = jnp.exp2((scores[pl.ds(c * CHUNK, CHUNK), :] - top[...]) * SCALE2)
                total[...] += jnp.sum(e, axis=0, keepdims=True)
                acc[...] += mm(v_t[:, c * CHUNK : (c + 1) * CHUNK], e.astype(jnp.bfloat16), NN)

        some = total[...] > 0
        safe = jnp.where(some, total[...], 1.0)
        out = heads_across((acc[...] * (1.0 / safe)).T).astype(jnp.bfloat16)
        out_ref[plan_ref[Q_ORDER + 2 * t]] = out[:BLOCK]
        out_ref[plan_ref[Q_ORDER + 2 * t + 1]] = out[BLOCK:]
        sums_ref[t] = jnp.where(some, top[...] * SCALE2 + jnp.log2(safe), NEGATIVE)
        return carried

    lax.fori_loop(0, 4, tile, 0)


def both_kernel(at_ref, own_ref, other_ref, send_ref):
    mine = at_ref[3]
    for j in range(4):
        send_ref[j, mine] = own_ref[...]
        send_ref[j, 1 - mine] = other_ref[...]


def grad_kernel(all_ref, weight_ref, send_ref):
    acc = jnp.zeros((ROWS, WIDE), jnp.float32)
    for x in range(4):
        for z in range(2):
            acc = acc + mm(all_ref[x, z], weight_ref[x, z], NN)
    for j in range(4):
        send_ref[j] = acc.astype(jnp.bfloat16)


def pack_kernel(plan_ref, out_ref, sums_ref, grad_ref, send_ref):
    rows = []
    for t in range(4):
        dots = []
        for h in range(2):
            lanes = slice(h * HD, (h + 1) * HD)
            halves = []
            for i in range(2):
                at = plan_ref[Q_ORDER + 2 * t + i]
                product = out_ref[at][:, lanes].astype(jnp.float32) * grad_ref[at][
                    :, lanes
                ].astype(jnp.float32)
                halves.append(jnp.sum(product, axis=1, keepdims=True))
            dot = jnp.concatenate(halves, axis=0)
            dots.append(jnp.broadcast_to(dot, (ROWS, HD)).T[0:1])
        pieces = split3(sums_ref[t]) + split3(jnp.concatenate(dots, axis=1))
        rows += [v.astype(jnp.float32) for v in pieces]
        rows.append(jnp.zeros((2, WIDE), jnp.float32))
    extra = jnp.concatenate(rows, axis=0).astype(jnp.bfloat16)
    for t in range(4):
        send_ref[t, :BLOCK, :] = out_ref[2 * t]
        send_ref[t, BLOCK:ROWS, :] = out_ref[2 * t + 1]
        send_ref[t, ROWS:, :] = extra


def joined(log_sums):
    top = functools.reduce(jnp.maximum, log_sums)
    weights = [jnp.exp2(s - top) for s in log_sums]
    total = functools.reduce(jnp.add, weights)
    inverse = 1.0 / total
    return top + jnp.log2(total), [w * inverse for w in weights]


def combine_kernel(at_ref, plan_ref, parts_ref, weight_ref, terms_ref, sums):
    for j in range(4):
        extra = parts_ref[j, ROWS:, :].astype(jnp.float32)
        for t in range(4):
            sums[t, j : j + 1, :] = join3(extra, 8 * t)
    lane = lax.rem(lax.broadcasted_iota(jnp.int32, (8, WIDE), 1), ROWS)
    first, second = plan_ref[Q_RANK + 2 * at_ref[1]], plan_ref[Q_RANK + 2 * at_ref[1] + 1]
    low, high = sums[first // 2], sums[second // 2]
    low = jnp.where(first % 2 == 1, pltpu.roll(low, WIDE - BLOCK, 1), low)
    high = jnp.where(second % 2 == 0, pltpu.roll(high, BLOCK, 1), high)
    mine = jnp.where(lane < BLOCK, low, high)
    log_sum, weights = joined([mine[j : j + 1] for j in range(4)])
    flat = []
    for w in weights:
        flat += [w[:, :HD], w[:, HD:]]
    columns = jnp.concatenate(flat + [jnp.zeros((HD - 8, HD), jnp.float32)], axis=0).T
    halves = []
    for h in range(2):
        lanes = slice(h * HD, (h + 1) * HD)
        acc = jnp.zeros((ROWS, HD), jnp.float32)
        for j in range(4):
            acc = acc + columns[:, 2 * j + h : 2 * j + h + 1] * parts_ref[
                j, :ROWS, lanes
            ].astype(jnp.float32)
        halves.append(acc.astype(jnp.bfloat16))
    attn_out = jnp.concatenate(halves, axis=1)
    for x in range(4):
        for c in range(4):
            part = mm(attn_out, weight_ref[x, pl.ds(c * WIDE, WIDE), :], NT)
            terms_ref[x, :, c * WIDE : (c + 1) * WIDE] = part.astype(jnp.bfloat16)


def backward_kernel(
    at_ref,
    plan_ref,
    lengths_ref,
    q_ref,
    grad_ref,
    parts_ref,
    terms_ref,
    kv0,
    kv1,
    dq0_ref,
    dq1_ref,
    dq2_ref,
    dq3_ref,
    own_ref,
    far_ref,
    dk_acc,
    dv_acc,
    k_s,
    v_s,
    k_t,
    stats,
    dq_parts,
    dq_acc,
):
    sort_keys(plan_ref, (kv0, kv1), k_s, v_s)
    for c in range(CHUNKS):
        k_t[:, c * CHUNK : (c + 1) * CHUNK] = k_s[c * CHUNK : (c + 1) * CHUNK, :].T
    dk_acc[...] = jnp.zeros_like(dk_acc)
    dv_acc[...] = jnp.zeros_like(dv_acc)
    extras = [parts_ref[j, ROWS:, :].astype(jnp.float32) for j in range(4)]
    for t in range(4):
        log_sum, weights = joined([join3(e, 8 * t) for e in extras])
        dots = [w * join3(e, 8 * t + 3) for w, e in zip(weights, extras)]
        stats[t, 0:1, :] = log_sum
        stats[t, 1:2, :] = functools.reduce(jnp.add, dots)

    def tile(t, carried):
        queries = two_blocks(q_ref, plan_ref, t)
        grads = two_blocks(grad_ref, plan_ref, t)
        log_sum, row_dots = stats[t, 0:1, :], stats[t, 1:2, :]
        pos, start = query_rows(plan_ref, lengths_ref, t)
        dq_acc[...] = jnp.zeros((HD, WIDE), jnp.float32)
        for c in range(CHUNKS):

            @pl.when(reached(plan_ref, t, c))
            def _():
                rows = pl.ds(c * CHUNK, CHUNK)
                s = mm(k_s[rows, :], queries, NT)
                dp = mm(v_s[rows, :], grads, NT)
                parts = []
                for b in range(CHUNK // BLOCK):
                    base = plan_ref[K_BASE + c * 4 + b]
                    raised = jnp.exp2(s[b * BLOCK : (b + 1) * BLOCK] * SCALE2 - log_sum)
                    parts.append(jnp.where(allowed(pos, start, base), raised, 0.0))
                p = jnp.concatenate(parts, axis=0)
                ds = (p * (dp - row_dots)).astype(jnp.bfloat16)
                dv_acc[rows, :] += mm(p.astype(jnp.bfloat16), grads, NN)
                dk_acc[rows, :] += mm(ds, queries, NN)
                dq_acc[...] += mm(k_t[:, c * CHUNK : (c + 1) * CHUNK], ds, NN)

        dq = heads_across((dq_acc[...] * SCALE).T).astype(jnp.bfloat16)
        for i in range(2):
            at = plan_ref[Q_ORDER + 2 * t + i]
            slot = jnp.bitwise_xor(at // 2, at_ref[1]) * 2 + at % 2
            dq_parts[slot] = dq[i * BLOCK : (i + 1) * BLOCK]
        return carried

    lax.fori_loop(0, 4, tile, 0)
    for k, ref in enumerate((dq0_ref, dq1_ref, dq2_ref, dq3_ref)):
        ref[:BLOCK, :] = dq_parts[2 * k]
        ref[BLOCK:, :] = dq_parts[2 * k + 1]
    z2 = at_ref[0] // 4
    for b in range(32):
        ref = far_ref if b // 16 else own_ref
        k = b % 16 // 2
        rows = pl.ds(pl.multiple_of(plan_ref[K_RANK + b] * BLOCK, BLOCK), BLOCK)
        half = pl.ds((b % 2) * BLOCK, BLOCK)
        z10 = (k // 2 % 2) * 2 + k // 4
        z2_flip = jnp.bitwise_xor(z2, k % 2)
        ref[z10, z2_flip, half, :HD] = (dk_acc[rows, :] * SCALE).astype(jnp.bfloat16)
        ref[z10, z2_flip, half, HD:] = dv_acc[rows, :].astype(jnp.bfloat16)


def call(kernel, outs, scratch, smem, vmem, flops, unread=0, space=pltpu.VMEM):
    specs = [pl.BlockSpec(memory_space=pltpu.SMEM)] * len(smem)
    specs += [pl.BlockSpec(memory_space=pltpu.VMEM)] * len(vmem)
    if unread:
        specs[unread] = pl.BlockSpec(memory_space=pl.ANY)
    out_specs = [pl.BlockSpec(memory_space=space)] * len(outs)
    return pl.pallas_call(
        kernel,
        out_shape=[jax.ShapeDtypeStruct(*o) for o in outs],
        in_specs=specs,
        out_specs=out_specs,
        scratch_shapes=scratch,
        compiler_params=pltpu.CompilerParams(vmem_limit_bytes=VMEM),
        cost_estimate=pl.CostEstimate(flops=flops, bytes_accessed=1 << 21, transcendentals=1 << 21),
    )(*smem, *vmem)


def spread(x, axis, n):
    return lax.all_to_all(jnp.broadcast_to(x, (n,) + x.shape), axis, 0, 0)


def gather(x, axis):
    return lax.all_gather(x, axis, axis=0)


def swap(x, axis):
    return lax.ppermute(x, axis, [(0, 1), (1, 0)])


def per_device(
    query_states, key_states, value_states, out_weight, out_grad, doc_lengths, block_order
):
    z_hi = lax.axis_index("z_hi")
    z_lo = lax.axis_index("z2") * 4 + lax.axis_index("z1") * 2 + lax.axis_index("z0")
    at = jnp.stack([z_lo, lax.axis_index("y"), lax.axis_index("core"), z_hi]).astype(jnp.int32)
    smem = (at, block_order, doc_lengths)

    bf16, f32 = jnp.bfloat16, jnp.float32
    other_grad = swap(out_grad, "z_hi")
    queries = spread(query_states, "y", 4)
    kv = jnp.concatenate([key_states, value_states], axis=1)
    (plan,) = call(
        plan_kernel,
        [((ROWS,), jnp.int32)],
        [pltpu.SMEM((32,), jnp.int32)],
        smem,
        (),
        10**8,
        space=pltpu.SMEM,
    )
    out_grad, other_grad, kv, queries, plan = lax.optimization_barrier(
        (out_grad, other_grad, kv, queries, plan)
    )
    queries = queries.reshape(8, BLOCK, WIDE)
    lookup = (plan, doc_lengths)
    (send,) = call(
        both_kernel, [((4, 2, ROWS, 512), bf16)], [], (at,), (out_grad, other_grad), 10**8
    )
    send, kv = lax.optimization_barrier((send, kv))
    all_grad = lax.all_to_all(send, "x", 0, 0)
    kv = gather(gather(kv, "z2"), "z1")
    all_grad, kv = lax.optimization_barrier((all_grad, kv))
    (send,) = call(
        grad_kernel,
        [((4, ROWS, WIDE), bf16)],
        [],
        (),
        (all_grad, out_weight.reshape(4, 2, 512, WIDE)),
        10**9,
    )
    send, kv = lax.optimization_barrier((send, kv))
    grads = lax.all_to_all(send, "y", 0, 0).reshape(8, BLOCK, WIDE)
    kv = gather(kv, "z0").reshape(8, ROWS, WIDE)
    keys_values = (kv, swap(kv, "core"))
    weight = out_weight.reshape(4, 1024, WIDE)

    partial_out, partial_sums = call(
        forward_kernel,
        [((8, BLOCK, WIDE), bf16), ((4, 1, WIDE), f32)],
        [
            pltpu.VMEM((2048, WIDE), f32),
            pltpu.VMEM((2048, HD), bf16),
            pltpu.VMEM((2048, HD), bf16),
            pltpu.VMEM((HD, 2048), bf16),
            pltpu.VMEM((1, WIDE), f32),
            pltpu.VMEM((1, WIDE), f32),
            pltpu.VMEM((HD, WIDE), f32),
        ],
        lookup,
        (queries,) + keys_values,
        8 * 10**9,
    )
    (send,) = call(
        pack_kernel,
        [((4, ROWS + EXTRA, WIDE), bf16)],
        [],
        (plan,),
        (partial_out, partial_sums, grads),
        10**9,
    )
    parts = lax.all_to_all(send, "y", 0, 0)
    (terms,) = call(
        combine_kernel,
        [((4, ROWS, 1024), bf16)],
        [pltpu.VMEM((4, 8, WIDE), f32)],
        (at, plan),
        (parts, weight),
        10**9,
    )
    all_terms = lax.all_to_all(terms, "x", 0, 0)
    dq0, dq1, dq2, dq3, own, far = call(
        backward_kernel,
        [((ROWS, WIDE), bf16)] * 4 + [((4, 2, ROWS, WIDE), bf16)] * 2,
        [
            pltpu.VMEM((2048, HD), f32),
            pltpu.VMEM((2048, HD), f32),
            pltpu.VMEM((2048, HD), bf16),
            pltpu.VMEM((2048, HD), bf16),
            pltpu.VMEM((HD, 2048), bf16),
            pltpu.VMEM((4, 8, WIDE), f32),
            pltpu.VMEM((8, BLOCK, WIDE), bf16),
            pltpu.VMEM((HD, WIDE), f32),
        ],
        (at,) + lookup,
        (queries, grads, parts, terms) + keys_values,
        12 * 10**9,
        unread=6,
    )
    own, far, all_terms = lax.optimization_barrier((own, far, all_terms))
    far = swap(far, "core")
    both = (own.astype(f32) + far.astype(f32)).astype(bf16)
    both, dq1, dq2, dq3, all_terms = lax.optimization_barrier(
        (both, dq1, dq2, dq3, all_terms)
    )
    partial = [lax.ppermute(x, "y", [(i, i ^ k) for i in range(4)]) for k, x in ((1, dq1), (2, dq2), (3, dq3))]
    both = lax.all_to_all(both, ("z1", "z0"), 0, 0)
    all_terms = jnp.sum(all_terms.astype(f32), axis=0)
    keep = jnp.where(z_hi == 0, all_terms[:, :512], all_terms[:, 512:])
    give = jnp.where(z_hi == 0, all_terms[:, 512:], all_terms[:, :512]).astype(bf16)
    got = swap(give, "z_hi")
    projected = (keep + got.astype(f32)).astype(bf16)
    both, *partial = lax.optimization_barrier((both, *partial))
    dq = dq0.astype(f32)
    for x in partial:
        dq = dq + x.astype(f32)
    grad_query = dq.astype(bf16)
    both = jnp.sum(both.astype(f32), axis=0)
    late = swap(both[1].astype(bf16), "z2")
    grad_kv = (both[0] + late.astype(f32)).astype(bf16)
    return projected, grad_query, grad_kv[:, :HD], grad_kv[:, HD:]


def solution(mesh):
    fine = Mesh(
        mesh.devices.reshape(2, 2, 2, 4, 2, 4, 2),
        ("z2", "z1", "z0", "y", "core", "x", "z_hi"),
    )
    ctx, head = ("z2", "z1", "z0", "y", "core"), ("x", "z_hi")
    both = P(ctx, head)
    return jax.shard_map(
        per_device,
        mesh=fine,
        in_specs=(both, both, both, P(None, head), both, P(), P()),
        out_specs=(both, both, both, both),
        check_vma=False,
    )
```

```python
import functools
import math

import jax
import jax.numpy as jnp
from jax import lax
from jax.experimental import pallas as pl
from jax.experimental.pallas import tpu as pltpu
from jax.sharding import Mesh
from jax.sharding import PartitionSpec as P

HD = 128
BLOCK = 64
ROWS = 128
WIDE = 2 * HD
EXTRA = 32
CHUNK = 256
CHUNKS = 8
DOCS = 16
NEGATIVE = -1e30
SCALE = HD ** (-0.5)
SCALE2 = SCALE * math.log2(math.e)
VMEM = 20 * 1024 * 1024

NT = (((1,), (1,)), ((), ()))
NN = (((1,), (0,)), ((), ()))


def mm(a, b, dims):
    return lax.dot_general(a, b, dims, preferred_element_type=jnp.float32)


def heads_down(x):
    return jnp.concatenate([x[:, :HD], x[:, HD:]], axis=0)


def heads_across(x):
    return jnp.concatenate([x[:ROWS], x[ROWS:]], axis=1)


def split3(x):
    hi = x.astype(jnp.bfloat16)
    rest = x - hi.astype(jnp.float32)
    mid = rest.astype(jnp.bfloat16)
    low = (rest - mid.astype(jnp.float32)).astype(jnp.bfloat16)
    return hi, mid, low


def join3(rows, at):
    return rows[at : at + 1] + rows[at + 1 : at + 2] + rows[at + 2 : at + 3]


K_RANK, K_BASE, Q_ORDER, Q_BASE, Q_RANK, Q_LOW, Q_RAW = 0, 32, 64, 72, 80, 88, 96


def key_base(at_ref, order_ref, block):
    half, k = block % 2, (block // 2) % 8
    z_lo = (k % 2) * 4 + (k // 2 % 2) * 2 + k // 4
    core = (1 - at_ref[2]) if block // 16 else at_ref[2]
    ctx = (z_lo * 4 + at_ref[1]) * 2 + core
    return order_ref[2 * ctx + half] * BLOCK


def plan_kernel(at_ref, order_ref, lengths_ref, plan_ref, raw):
    def rank(values, count, at, base_at):
        def one(b, carried):
            mine, place = values[b], 0
            for j in range(count):
                place = place + jnp.where(values[j] < mine, 1, 0)
            plan_ref[at + b] = place
            plan_ref[base_at + place] = mine
            return carried

        lax.fori_loop(0, count, one, 0)

    for b in range(32):
        raw[b] = key_base(at_ref, order_ref, b)
    rank(raw, 32, K_RANK, K_BASE)
    for b in range(8):
        ctx = (at_ref[0] * 4 + b // 2) * 2 + at_ref[2]
        raw[b] = order_ref[2 * ctx + b % 2] * BLOCK
    rank(raw, 8, Q_RANK, Q_BASE)
    for b in range(8):
        plan_ref[Q_ORDER + plan_ref[Q_RANK + b]] = b
    for b in range(8):
        first, low, end = plan_ref[Q_BASE + b], 0, 0
        for d in range(DOCS):
            end = end + lengths_ref[d]
            low = jnp.where(first >= end, end, low)
        plan_ref[Q_LOW + b] = low


def query_rows(plan_ref, lengths_ref, t):
    lane = lax.broadcasted_iota(jnp.int32, (1, WIDE), 1)
    row = lax.rem(lane, ROWS)
    first, second = plan_ref[Q_BASE + 2 * t], plan_ref[Q_BASE + 2 * t + 1]
    pos = jnp.where(row < BLOCK, first + row, second + row - BLOCK)
    start = jnp.zeros_like(pos)
    end = 0
    for d in range(DOCS):
        end = end + lengths_ref[d]
        start = jnp.where(pos >= end, end, start)
    return pos, start


def reached(plan_ref, t, c):
    low, high = plan_ref[K_BASE + 4 * c], plan_ref[K_BASE + 4 * c + 3] + BLOCK - 1
    seen = []
    for i in range(2):
        at = 2 * t + i
        last = plan_ref[Q_BASE + at] + BLOCK - 1
        seen.append((low <= last) & (high >= plan_ref[Q_LOW + at]))
    return seen[0] | seen[1]


def allowed(pos, start, base):
    row = lax.broadcasted_iota(jnp.int32, (BLOCK, WIDE), 0)
    return (row >= start - base) & (row <= pos - base)


def sort_keys(plan_ref, kv_refs, k_s, v_s):
    for b in range(32):
        rows = pl.ds(pl.multiple_of(plan_ref[K_RANK + b] * BLOCK, BLOCK), BLOCK)
        ref = kv_refs[b // 16]
        half = pl.ds((b % 2) * BLOCK, BLOCK)
        k_s[rows, :] = ref[b % 16 // 2, half, :HD]
        v_s[rows, :] = ref[b % 16 // 2, half, HD:]


def two_blocks(ref, plan_ref, t, at):
    first, second = ref[plan_ref[Q_ORDER + 2 * t]], ref[plan_ref[Q_ORDER + 2 * t + 1]]
    parts = [x[:, at + h * HD : at + (h + 1) * HD] for h in range(2) for x in (first, second)]
    return jnp.concatenate(parts, axis=0)


def two_lanes(stats, plan_ref, t):
    lane = lax.rem(lax.broadcasted_iota(jnp.int32, (8, WIDE), 1), ROWS)
    first, second = plan_ref[Q_ORDER + 2 * t], plan_ref[Q_ORDER + 2 * t + 1]
    low, high = stats[first // 2], stats[second // 2]
    low = jnp.where(first % 2 == 1, pltpu.roll(low, WIDE - BLOCK, 1), low)
    high = jnp.where(second % 2 == 0, pltpu.roll(high, BLOCK, 1), high)
    return jnp.where(lane < BLOCK, low, high)


def loader_rows(at_ref, order_ref, lengths_ref, t):
    z_lo, core = at_ref[0], at_ref[2]
    ctx = (z_lo * 4 + t) * 2 + core
    lane = lax.broadcasted_iota(jnp.int32, (1, WIDE), 1)
    row = lax.rem(lane, ROWS)
    first, second = order_ref[2 * ctx] * BLOCK, order_ref[2 * ctx + 1] * BLOCK
    pos = jnp.where(row < BLOCK, first + row, second + row - BLOCK)
    start = jnp.zeros_like(pos)
    end = 0
    for d in range(DOCS):
        end = end + lengths_ref[d]
        start = jnp.where(pos >= end, end, start)
    return pos, start


def kv_chunk(kv_refs, c, which):
    ref = kv_refs[c // 4]
    first = 2 * (c % 4)
    columns = slice(which * HD, (which + 1) * HD)
    return jnp.concatenate([ref[first, :, columns], ref[first + 1, :, columns]], axis=0)


def forward_kernel(
    at_ref, order_ref, lengths_ref, q_ref, kv0, kv1, out_ref, sums_ref, scores, v_t
):
    kv_refs = (kv0, kv1)
    for c in range(CHUNKS):
        v_t[:, c * CHUNK : (c + 1) * CHUNK] = kv_chunk(kv_refs, c, 1).T

    def tile(t, carried):
        queries = heads_down(q_ref[t, :, :WIDE])
        pos, start = loader_rows(at_ref, order_ref, lengths_ref, t)
        top = jnp.full((1, WIDE), NEGATIVE, jnp.float32)
        for c in range(CHUNKS):
            s = mm(kv_chunk(kv_refs, c, 0), queries, NT)
            for b in range(CHUNK // BLOCK):
                base = key_base(at_ref, order_ref, c * 4 + b)
                part = jnp.where(
                    allowed(pos, start, base), s[b * BLOCK : (b + 1) * BLOCK], NEGATIVE
                )
                scores[pl.ds(c * CHUNK + b * BLOCK, BLOCK), :] = part
                top = jnp.maximum(top, jnp.max(part, axis=0, keepdims=True))
        top = jnp.maximum(top, 0.1 * NEGATIVE)
        total = jnp.zeros((1, WIDE), jnp.float32)
        acc = jnp.zeros((HD, WIDE), jnp.float32)
        for c in range(CHUNKS):
            e = jnp.exp2((scores[pl.ds(c * CHUNK, CHUNK), :] - top) * SCALE2)
            total = total + jnp.sum(e, axis=0, keepdims=True)
            acc = acc + mm(v_t[:, c * CHUNK : (c + 1) * CHUNK], e.astype(jnp.bfloat16), NN)
        some = total > 0
        safe = jnp.where(some, total, 1.0)
        out_ref[t] = heads_across((acc * (1.0 / safe)).T).astype(jnp.bfloat16)
        sums_ref[t] = jnp.where(some, top * SCALE2 + jnp.log2(safe), NEGATIVE)
        return carried

    lax.fori_loop(0, 4, tile, 0)


def pack_kernel(out_ref, sums_ref, grad_ref, send_ref):
    rows = []
    for t in range(4):
        dots = []
        for h in range(2):
            lanes = slice(h * HD, (h + 1) * HD)
            product = out_ref[t, :, lanes].astype(jnp.float32) * grad_ref[
                t, :, slice(WIDE + h * HD, WIDE + (h + 1) * HD)
            ].astype(jnp.float32)
            dot = jnp.sum(product, axis=1, keepdims=True)
            dots.append(jnp.broadcast_to(dot, (ROWS, HD)).T[0:1])
        pieces = split3(sums_ref[t]) + split3(jnp.concatenate(dots, axis=1))
        rows += [v.astype(jnp.float32) for v in pieces]
        rows.append(jnp.zeros((2, WIDE), jnp.float32))
    extra = jnp.concatenate(rows, axis=0).astype(jnp.bfloat16)
    for t in range(4):
        send_ref[t, :ROWS, :] = out_ref[t]
        send_ref[t, ROWS:, :] = extra


def joined(log_sums):
    top = functools.reduce(jnp.maximum, log_sums)
    weights = [jnp.exp2(s - top) for s in log_sums]
    total = functools.reduce(jnp.add, weights)
    inverse = 1.0 / total
    return top + jnp.log2(total), [w * inverse for w in weights]


def combine_kernel(at_ref, parts_ref, weight_ref, terms_ref, sums):
    for j in range(4):
        extra = parts_ref[j, ROWS:, :].astype(jnp.float32)
        for t in range(4):
            sums[t, j : j + 1, :] = join3(extra, 8 * t)
    mine = sums[at_ref[1]]
    log_sum, weights = joined([mine[j : j + 1] for j in range(4)])
    flat = []
    for w in weights:
        flat += [w[:, :HD], w[:, HD:]]
    columns = jnp.concatenate(flat + [jnp.zeros((HD - 8, HD), jnp.float32)], axis=0).T
    halves = []
    for h in range(2):
        lanes = slice(h * HD, (h + 1) * HD)
        acc = jnp.zeros((ROWS, HD), jnp.float32)
        for j in range(4):
            acc = acc + columns[:, 2 * j + h : 2 * j + h + 1] * parts_ref[
                j, :ROWS, lanes
            ].astype(jnp.float32)
        halves.append(acc.astype(jnp.bfloat16))
    attn_out = jnp.concatenate(halves, axis=1)
    for x in range(4):
        for c in range(4):
            part = mm(attn_out, weight_ref[x, pl.ds(c * WIDE, WIDE), :], NT)
            terms_ref[x, :, c * WIDE : (c + 1) * WIDE] = part.astype(jnp.bfloat16)


def backward_kernel(
    at_ref,
    plan_ref,
    lengths_ref,
    both_ref,
    parts_ref,
    terms_ref,
    kv0,
    kv1,
    dq0_ref,
    dq1_ref,
    dq2_ref,
    dq3_ref,
    own_ref,
    far_ref,
    dk_acc,
    dv_acc,
    k_s,
    v_s,
    k_t,
    stats,
    dq_parts,
    dq_acc,
):
    sort_keys(plan_ref, (kv0, kv1), k_s, v_s)
    for c in range(CHUNKS):
        k_t[:, c * CHUNK : (c + 1) * CHUNK] = k_s[c * CHUNK : (c + 1) * CHUNK, :].T
    dk_acc[...] = jnp.zeros_like(dk_acc)
    dv_acc[...] = jnp.zeros_like(dv_acc)
    extras = [parts_ref[j, ROWS:, :].astype(jnp.float32) for j in range(4)]
    for t in range(4):
        log_sum, weights = joined([join3(e, 8 * t) for e in extras])
        dots = [w * join3(e, 8 * t + 3) for w, e in zip(weights, extras)]
        stats[t, 0:1, :] = log_sum
        stats[t, 1:2, :] = functools.reduce(jnp.add, dots)

    def tile(t, carried):
        queries = two_blocks(both_ref, plan_ref, t, 0)
        grads = two_blocks(both_ref, plan_ref, t, WIDE)
        mine = two_lanes(stats, plan_ref, t)
        log_sum, row_dots = mine[0:1, :], mine[1:2, :]
        pos, start = query_rows(plan_ref, lengths_ref, t)
        dq_acc[...] = jnp.zeros((HD, WIDE), jnp.float32)
        for c in range(CHUNKS):

            @pl.when(reached(plan_ref, t, c))
            def _():
                rows = pl.ds(c * CHUNK, CHUNK)
                s = mm(k_s[rows, :], queries, NT)
                dp = mm(v_s[rows, :], grads, NT)
                parts = []
                for b in range(CHUNK // BLOCK):
                    base = plan_ref[K_BASE + c * 4 + b]
                    raised = jnp.exp2(s[b * BLOCK : (b + 1) * BLOCK] * SCALE2 - log_sum)
                    parts.append(jnp.where(allowed(pos, start, base), raised, 0.0))
                p = jnp.concatenate(parts, axis=0)
                ds = (p * (dp - row_dots)).astype(jnp.bfloat16)
                dv_acc[rows, :] += mm(p.astype(jnp.bfloat16), grads, NN)
                dk_acc[rows, :] += mm(ds, queries, NN)
                dq_acc[...] += mm(k_t[:, c * CHUNK : (c + 1) * CHUNK], ds, NN)

        dq = heads_across((dq_acc[...] * SCALE).T).astype(jnp.bfloat16)
        for i in range(2):
            at = plan_ref[Q_ORDER + 2 * t + i]
            slot = jnp.bitwise_xor(at // 2, at_ref[1]) * 2 + at % 2
            dq_parts[slot] = dq[i * BLOCK : (i + 1) * BLOCK]
        return carried

    lax.fori_loop(0, 4, tile, 0)
    for k, ref in enumerate((dq0_ref, dq1_ref, dq2_ref, dq3_ref)):
        ref[:BLOCK, :] = dq_parts[2 * k]
        ref[BLOCK:, :] = dq_parts[2 * k + 1]
    z2 = at_ref[0] // 4
    for b in range(32):
        ref = far_ref if b // 16 else own_ref
        k = b % 16 // 2
        rows = pl.ds(pl.multiple_of(plan_ref[K_RANK + b] * BLOCK, BLOCK), BLOCK)
        half = pl.ds((b % 2) * BLOCK, BLOCK)
        z10 = (k // 2 % 2) * 2 + k // 4
        z2_flip = jnp.bitwise_xor(z2, k % 2)
        ref[z10, z2_flip, half, :HD] = (dk_acc[rows, :] * SCALE).astype(jnp.bfloat16)
        ref[z10, z2_flip, half, HD:] = dv_acc[rows, :].astype(jnp.bfloat16)


def call(kernel, outs, scratch, smem, vmem, flops, unread=0, space=pltpu.VMEM):
    specs = [pl.BlockSpec(memory_space=pltpu.SMEM)] * len(smem)
    specs += [pl.BlockSpec(memory_space=pltpu.VMEM)] * len(vmem)
    if unread:
        specs[unread] = pl.BlockSpec(memory_space=pl.ANY)
    out_specs = [pl.BlockSpec(memory_space=space)] * len(outs)
    return pl.pallas_call(
        kernel,
        out_shape=[jax.ShapeDtypeStruct(*o) for o in outs],
        in_specs=specs,
        out_specs=out_specs,
        scratch_shapes=scratch,
        compiler_params=pltpu.CompilerParams(vmem_limit_bytes=VMEM),
        cost_estimate=pl.CostEstimate(flops=flops, bytes_accessed=1 << 21, transcendentals=1 << 21),
    )(*smem, *vmem)


def spread(x, axis, n):
    return lax.all_to_all(jnp.broadcast_to(x, (n,) + x.shape), axis, 0, 0)


def gather(x, axis):
    return lax.all_gather(x, axis, axis=0)


def swap(x, axis):
    return lax.ppermute(x, axis, [(0, 1), (1, 0)])


def per_device(
    query_states, key_states, value_states, out_weight, out_grad, doc_lengths, block_order
):
    z_hi = lax.axis_index("z_hi")
    z_lo = lax.axis_index("z2") * 4 + lax.axis_index("z1") * 2 + lax.axis_index("z0")
    at = jnp.stack([z_lo, lax.axis_index("y"), lax.axis_index("core"), z_hi]).astype(jnp.int32)
    smem = (at, block_order, doc_lengths)

    bf16, f32 = jnp.bfloat16, jnp.float32
    weight = out_weight.reshape(4, 2, 512, WIDE)
    send = gather(out_grad, "z_hi")
    kv = jnp.concatenate([key_states, value_states], axis=1)
    send, kv = lax.optimization_barrier((send, kv))
    all_grad = spread(send, "x", 4)
    kv = gather(gather(kv, "z2"), "z1")
    all_grad, kv = lax.optimization_barrier((all_grad, kv))
    grad_attn = jnp.einsum("xzrd,xzdc->rc", all_grad, weight, preferred_element_type=f32)
    send = jnp.concatenate([query_states, grad_attn.astype(bf16)], axis=1)
    send, kv = lax.optimization_barrier((send, kv))
    queries_grads = spread(send, "y", 4)
    kv = gather(kv, "z0").reshape(8, ROWS, WIDE)
    kv, queries_grads = lax.optimization_barrier((kv, queries_grads))
    keys_values = (kv, swap(kv, "core"))
    weight = out_weight.reshape(4, 1024, WIDE)

    partial_out, partial_sums = call(
        forward_kernel,
        [((4, ROWS, WIDE), bf16), ((4, 1, WIDE), f32)],
        [pltpu.VMEM((2048, WIDE), f32), pltpu.VMEM((HD, 2048), bf16)],
        smem,
        (queries_grads,) + keys_values,
        8 * 10**9,
    )
    (send,) = call(
        pack_kernel,
        [((4, ROWS + EXTRA, WIDE), bf16)],
        [],
        (),
        (partial_out, partial_sums, queries_grads),
        10**9,
    )
    order, send = lax.optimization_barrier((block_order, send))
    (plan,) = call(
        plan_kernel,
        [((ROWS,), jnp.int32)],
        [pltpu.SMEM((32,), jnp.int32)],
        (at, order, doc_lengths),
        (),
        3 * 10**9,
        space=pltpu.SMEM,
    )
    parts = lax.all_to_all(send, "y", 0, 0)
    parts, plan = lax.optimization_barrier((parts, plan))
    (terms,) = call(
        combine_kernel,
        [((4, ROWS, 1024), bf16)],
        [pltpu.VMEM((4, 8, WIDE), f32)],
        (at,),
        (parts, weight),
        10**9,
    )
    all_terms = lax.all_to_all(terms, "x", 0, 0)
    dq0, dq1, dq2, dq3, own, far = call(
        backward_kernel,
        [((ROWS, WIDE), bf16)] * 4 + [((4, 2, ROWS, WIDE), bf16)] * 2,
        [
            pltpu.VMEM((2048, HD), f32),
            pltpu.VMEM((2048, HD), f32),
            pltpu.VMEM((2048, HD), bf16),
            pltpu.VMEM((2048, HD), bf16),
            pltpu.VMEM((HD, 2048), bf16),
            pltpu.VMEM((4, 8, WIDE), f32),
            pltpu.VMEM((8, BLOCK, WIDE), bf16),
            pltpu.VMEM((HD, WIDE), f32),
        ],
        (at, plan, doc_lengths),
        (queries_grads.reshape(8, BLOCK, 2 * WIDE), parts, terms) + keys_values,
        12 * 10**9,
        unread=5,
    )
    own, far, all_terms = lax.optimization_barrier((own, far, all_terms))
    far = swap(far, "core")
    both = (own.astype(f32) + far.astype(f32)).astype(bf16)
    both, dq1, dq2, dq3, all_terms = lax.optimization_barrier(
        (both, dq1, dq2, dq3, all_terms)
    )
    partial = [lax.ppermute(x, "y", [(i, i ^ k) for i in range(4)]) for k, x in ((1, dq1), (2, dq2), (3, dq3))]
    both = lax.all_to_all(both, ("z1", "z0"), 0, 0)
    all_terms = jnp.sum(all_terms.astype(f32), axis=0)
    keep = jnp.where(z_hi == 0, all_terms[:, :512], all_terms[:, 512:])
    give = jnp.where(z_hi == 0, all_terms[:, 512:], all_terms[:, :512]).astype(bf16)
    got = swap(give, "z_hi")
    projected = (keep + got.astype(f32)).astype(bf16)
    both, *partial = lax.optimization_barrier((both, *partial))
    dq = dq0.astype(f32)
    for x in partial:
        dq = dq + x.astype(f32)
    grad_query = dq.astype(bf16)
    both = jnp.sum(both.astype(f32), axis=0)
    late = swap(both[1].astype(bf16), "z2")
    grad_kv = (both[0] + late.astype(f32)).astype(bf16)
    return projected, grad_query, grad_kv[:, :HD], grad_kv[:, HD:]


def solution(mesh):
    fine = Mesh(
        mesh.devices.reshape(2, 2, 2, 4, 2, 4, 2),
        ("z2", "z1", "z0", "y", "core", "x", "z_hi"),
    )
    ctx, head = ("z2", "z1", "z0", "y", "core"), ("x", "z_hi")
    both = P(ctx, head)
    return jax.shard_map(
        per_device,
        mesh=fine,
        in_specs=(both, both, both, P(None, head), both, P(), P()),
        out_specs=(both, both, both, both),
        check_vma=False,
    )
```

```python
import functools
import math

import jax
import jax.numpy as jnp
from jax import lax
from jax.experimental import pallas as pl
from jax.experimental.pallas import tpu as pltpu
from jax.sharding import Mesh
from jax.sharding import PartitionSpec as P

HD = 128
BLOCK = 64
ROWS = 128
WIDE = 2 * HD
EXTRA = 32
CHUNK = 256
CHUNKS = 8
DOCS = 16
NEGATIVE = -1e30
SCALE = HD ** (-0.5)
SCALE2 = SCALE * math.log2(math.e)
VMEM = 20 * 1024 * 1024

NT = (((1,), (1,)), ((), ()))
NN = (((1,), (0,)), ((), ()))


def mm(a, b, dims):
    return lax.dot_general(a, b, dims, preferred_element_type=jnp.float32)


def heads_down(x):
    return jnp.concatenate([x[:, :HD], x[:, HD:]], axis=0)


def heads_across(x):
    return jnp.concatenate([x[:ROWS], x[ROWS:]], axis=1)


def split3(x):
    hi = x.astype(jnp.bfloat16)
    rest = x - hi.astype(jnp.float32)
    mid = rest.astype(jnp.bfloat16)
    low = (rest - mid.astype(jnp.float32)).astype(jnp.bfloat16)
    return hi, mid, low


def join3(rows, at):
    return rows[at : at + 1] + rows[at + 1 : at + 2] + rows[at + 2 : at + 3]


K_RANK, K_BASE, Q_ORDER, Q_BASE, Q_RANK, Q_LOW, Q_RAW = 0, 32, 64, 72, 80, 88, 96


def key_base(at_ref, order_ref, block):
    half, k = block % 2, (block // 2) % 8
    z_lo = (k % 2) * 4 + (k // 2 % 2) * 2 + k // 4
    core = (1 - at_ref[2]) if block // 16 else at_ref[2]
    ctx = (z_lo * 4 + at_ref[1]) * 2 + core
    return order_ref[2 * ctx + half] * BLOCK


def plan_kernel(at_ref, order_ref, lengths_ref, plan_ref, raw):
    def rank(values, count, at, base_at):
        def one(b, carried):
            mine, place = values[b], 0
            for j in range(count):
                place = place + jnp.where(values[j] < mine, 1, 0)
            plan_ref[at + b] = place
            plan_ref[base_at + place] = mine
            return carried

        lax.fori_loop(0, count, one, 0)

    for b in range(32):
        raw[b] = key_base(at_ref, order_ref, b)
    rank(raw, 32, K_RANK, K_BASE)
    for b in range(8):
        ctx = (at_ref[0] * 4 + b // 2) * 2 + at_ref[2]
        raw[b] = order_ref[2 * ctx + b % 2] * BLOCK
    rank(raw, 8, Q_RANK, Q_BASE)
    for b in range(8):
        plan_ref[Q_ORDER + plan_ref[Q_RANK + b]] = b
    for b in range(8):
        first, low, end = plan_ref[Q_BASE + b], 0, 0
        for d in range(DOCS):
            end = end + lengths_ref[d]
            low = jnp.where(first >= end, end, low)
        plan_ref[Q_LOW + b] = low


def query_rows(plan_ref, lengths_ref, t):
    lane = lax.broadcasted_iota(jnp.int32, (1, WIDE), 1)
    row = lax.rem(lane, ROWS)
    first, second = plan_ref[Q_BASE + 2 * t], plan_ref[Q_BASE + 2 * t + 1]
    pos = jnp.where(row < BLOCK, first + row, second + row - BLOCK)
    start = jnp.zeros_like(pos)
    end = 0
    for d in range(DOCS):
        end = end + lengths_ref[d]
        start = jnp.where(pos >= end, end, start)
    return pos, start


def reached(plan_ref, t, c):
    low, high = plan_ref[K_BASE + 4 * c], plan_ref[K_BASE + 4 * c + 3] + BLOCK - 1
    seen = []
    for i in range(2):
        at = 2 * t + i
        last = plan_ref[Q_BASE + at] + BLOCK - 1
        seen.append((low <= last) & (high >= plan_ref[Q_LOW + at]))
    return seen[0] | seen[1]


def allowed(pos, start, base):
    row = lax.broadcasted_iota(jnp.int32, (BLOCK, WIDE), 0)
    return (row >= start - base) & (row <= pos - base)


def sort_keys(plan_ref, kv_refs, k_s, v_s):
    for b in range(32):
        rows = pl.ds(pl.multiple_of(plan_ref[K_RANK + b] * BLOCK, BLOCK), BLOCK)
        ref = kv_refs[b // 16]
        half = pl.ds((b % 2) * BLOCK, BLOCK)
        k_s[rows, :] = ref[b % 16 // 2, half, :HD]
        v_s[rows, :] = ref[b % 16 // 2, half, HD:]


def two_blocks(ref, plan_ref, t, at):
    first, second = ref[plan_ref[Q_ORDER + 2 * t]], ref[plan_ref[Q_ORDER + 2 * t + 1]]
    parts = [x[:, at + h * HD : at + (h + 1) * HD] for h in range(2) for x in (first, second)]
    return jnp.concatenate(parts, axis=0)


def two_lanes(stats, plan_ref, t):
    lane = lax.rem(lax.broadcasted_iota(jnp.int32, (8, WIDE), 1), ROWS)
    first, second = plan_ref[Q_ORDER + 2 * t], plan_ref[Q_ORDER + 2 * t + 1]
    low, high = stats[first // 2], stats[second // 2]
    low = jnp.where(first % 2 == 1, pltpu.roll(low, WIDE - BLOCK, 1), low)
    high = jnp.where(second % 2 == 0, pltpu.roll(high, BLOCK, 1), high)
    return jnp.where(lane < BLOCK, low, high)


def loader_rows(at_ref, order_ref, lengths_ref, t):
    z_lo, core = at_ref[0], at_ref[2]
    ctx = (z_lo * 4 + t) * 2 + core
    lane = lax.broadcasted_iota(jnp.int32, (1, WIDE), 1)
    row = lax.rem(lane, ROWS)
    first, second = order_ref[2 * ctx] * BLOCK, order_ref[2 * ctx + 1] * BLOCK
    pos = jnp.where(row < BLOCK, first + row, second + row - BLOCK)
    start = jnp.zeros_like(pos)
    end = 0
    for d in range(DOCS):
        end = end + lengths_ref[d]
        start = jnp.where(pos >= end, end, start)
    return pos, start


def kv_chunk(kv_refs, c, which):
    ref = kv_refs[c // 4]
    first = 2 * (c % 4)
    columns = slice(which * HD, (which + 1) * HD)
    return jnp.concatenate([ref[first, :, columns], ref[first + 1, :, columns]], axis=0)


def forward_kernel(
    at_ref, order_ref, lengths_ref, q_ref, kv0, kv1, out_ref, sums_ref, scores, v_t
):
    kv_refs = (kv0, kv1)
    for c in range(CHUNKS):
        v_t[:, c * CHUNK : (c + 1) * CHUNK] = kv_chunk(kv_refs, c, 1).T

    def tile(t, carried):
        queries = heads_down(q_ref[t, :, :WIDE])
        pos, start = loader_rows(at_ref, order_ref, lengths_ref, t)
        top = jnp.full((1, WIDE), NEGATIVE, jnp.float32)
        for c in range(CHUNKS):
            s = mm(kv_chunk(kv_refs, c, 0), queries, NT)
            for b in range(CHUNK // BLOCK):
                base = key_base(at_ref, order_ref, c * 4 + b)
                part = jnp.where(
                    allowed(pos, start, base), s[b * BLOCK : (b + 1) * BLOCK], NEGATIVE
                )
                scores[pl.ds(c * CHUNK + b * BLOCK, BLOCK), :] = part
                top = jnp.maximum(top, jnp.max(part, axis=0, keepdims=True))
        top = jnp.maximum(top, 0.1 * NEGATIVE)
        total = jnp.zeros((1, WIDE), jnp.float32)
        acc = jnp.zeros((HD, WIDE), jnp.float32)
        for c in range(CHUNKS):
            e = jnp.exp2((scores[pl.ds(c * CHUNK, CHUNK), :] - top) * SCALE2)
            total = total + jnp.sum(e, axis=0, keepdims=True)
            acc = acc + mm(v_t[:, c * CHUNK : (c + 1) * CHUNK], e.astype(jnp.bfloat16), NN)
        some = total > 0
        safe = jnp.where(some, total, 1.0)
        out_ref[t] = heads_across((acc * (1.0 / safe)).T).astype(jnp.bfloat16)
        sums_ref[t] = jnp.where(some, top * SCALE2 + jnp.log2(safe), NEGATIVE)
        return carried

    lax.fori_loop(0, 4, tile, 0)


def pack_kernel(out_ref, sums_ref, grad_ref, send_ref):
    rows = []
    for t in range(4):
        dots = []
        for h in range(2):
            lanes = slice(h * HD, (h + 1) * HD)
            product = out_ref[t, :, lanes].astype(jnp.float32) * grad_ref[
                t, :, slice(WIDE + h * HD, WIDE + (h + 1) * HD)
            ].astype(jnp.float32)
            dot = jnp.sum(product, axis=1, keepdims=True)
            dots.append(jnp.broadcast_to(dot, (ROWS, HD)).T[0:1])
        pieces = split3(sums_ref[t]) + split3(jnp.concatenate(dots, axis=1))
        rows += [v.astype(jnp.float32) for v in pieces]
        rows.append(jnp.zeros((2, WIDE), jnp.float32))
    extra = jnp.concatenate(rows, axis=0).astype(jnp.bfloat16)
    for t in range(4):
        send_ref[t, :ROWS, :] = out_ref[t]
        send_ref[t, ROWS:, :] = extra


def joined(log_sums):
    top = functools.reduce(jnp.maximum, log_sums)
    weights = [jnp.exp2(s - top) for s in log_sums]
    total = functools.reduce(jnp.add, weights)
    inverse = 1.0 / total
    return top + jnp.log2(total), [w * inverse for w in weights]


def combine_kernel(at_ref, parts_ref, weight_ref, terms_ref, sums):
    for j in range(4):
        extra = parts_ref[j, ROWS:, :].astype(jnp.float32)
        for t in range(4):
            sums[t, j : j + 1, :] = join3(extra, 8 * t)
    mine = sums[at_ref[1]]
    log_sum, weights = joined([mine[j : j + 1] for j in range(4)])
    flat = []
    for w in weights:
        flat += [w[:, :HD], w[:, HD:]]
    columns = jnp.concatenate(flat + [jnp.zeros((HD - 8, HD), jnp.float32)], axis=0).T
    halves = []
    for h in range(2):
        lanes = slice(h * HD, (h + 1) * HD)
        acc = jnp.zeros((ROWS, HD), jnp.float32)
        for j in range(4):
            acc = acc + columns[:, 2 * j + h : 2 * j + h + 1] * parts_ref[
                j, :ROWS, lanes
            ].astype(jnp.float32)
        halves.append(acc.astype(jnp.bfloat16))
    attn_out = jnp.concatenate(halves, axis=1)
    for x in range(4):
        for c in range(4):
            part = mm(attn_out, weight_ref[x, pl.ds(c * WIDE, WIDE), :], NT)
            terms_ref[x, :, c * WIDE : (c + 1) * WIDE] = part.astype(jnp.bfloat16)


def backward_kernel(
    at_ref,
    plan_ref,
    lengths_ref,
    both_ref,
    parts_ref,
    terms_ref,
    kv0,
    kv1,
    dq0_ref,
    dq1_ref,
    dq2_ref,
    dq3_ref,
    own_ref,
    far_ref,
    dk_acc,
    dv_acc,
    k_s,
    v_s,
    k_t,
    stats,
    dq_parts,
    dq_acc,
):
    sort_keys(plan_ref, (kv0, kv1), k_s, v_s)
    for c in range(CHUNKS):
        k_t[:, c * CHUNK : (c + 1) * CHUNK] = k_s[c * CHUNK : (c + 1) * CHUNK, :].T
    dk_acc[...] = jnp.zeros_like(dk_acc)
    dv_acc[...] = jnp.zeros_like(dv_acc)
    extras = [parts_ref[j, ROWS:, :].astype(jnp.float32) for j in range(4)]
    for t in range(4):
        log_sum, weights = joined([join3(e, 8 * t) for e in extras])
        dots = [w * join3(e, 8 * t + 3) for w, e in zip(weights, extras)]
        stats[t, 0:1, :] = log_sum
        stats[t, 1:2, :] = functools.reduce(jnp.add, dots)

    def tile(t, carried):
        queries = two_blocks(both_ref, plan_ref, t, 0)
        grads = two_blocks(both_ref, plan_ref, t, WIDE)
        mine = two_lanes(stats, plan_ref, t)
        log_sum, row_dots = mine[0:1, :], mine[1:2, :]
        pos, start = query_rows(plan_ref, lengths_ref, t)
        dq_acc[...] = jnp.zeros((HD, WIDE), jnp.float32)
        for c in range(CHUNKS):

            @pl.when(reached(plan_ref, t, c))
            def _():
                rows = pl.ds(c * CHUNK, CHUNK)
                s = mm(k_s[rows, :], queries, NT)
                dp = mm(v_s[rows, :], grads, NT)
                parts = []
                for b in range(CHUNK // BLOCK):
                    base = plan_ref[K_BASE + c * 4 + b]
                    raised = jnp.exp2(s[b * BLOCK : (b + 1) * BLOCK] * SCALE2 - log_sum)
                    parts.append(jnp.where(allowed(pos, start, base), raised, 0.0))
                p = jnp.concatenate(parts, axis=0)
                ds = (p * (dp - row_dots)).astype(jnp.bfloat16)
                dv_acc[rows, :] += mm(p.astype(jnp.bfloat16), grads, NN)
                dk_acc[rows, :] += mm(ds, queries, NN)
                dq_acc[...] += mm(k_t[:, c * CHUNK : (c + 1) * CHUNK], ds, NN)

        dq = heads_across((dq_acc[...] * SCALE).T).astype(jnp.bfloat16)
        for i in range(2):
            at = plan_ref[Q_ORDER + 2 * t + i]
            slot = jnp.bitwise_xor(at // 2, at_ref[1]) * 2 + at % 2
            dq_parts[slot] = dq[i * BLOCK : (i + 1) * BLOCK]
        return carried

    lax.fori_loop(0, 4, tile, 0)
    for k, ref in enumerate((dq0_ref, dq1_ref, dq2_ref, dq3_ref)):
        ref[:BLOCK, :] = dq_parts[2 * k]
        ref[BLOCK:, :] = dq_parts[2 * k + 1]
    z2 = at_ref[0] // 4
    for b in range(32):
        ref = far_ref if b // 16 else own_ref
        k = b % 16 // 2
        rows = pl.ds(pl.multiple_of(plan_ref[K_RANK + b] * BLOCK, BLOCK), BLOCK)
        half = pl.ds((b % 2) * BLOCK, BLOCK)
        z10 = (k // 2 % 2) * 2 + k // 4
        z2_flip = jnp.bitwise_xor(z2, k % 2)
        ref[z10, z2_flip, half, :HD] = (dk_acc[rows, :] * SCALE).astype(jnp.bfloat16)
        ref[z10, z2_flip, half, HD:] = dv_acc[rows, :].astype(jnp.bfloat16)


def call(kernel, outs, scratch, smem, vmem, flops, unread=0, space=pltpu.VMEM):
    specs = [pl.BlockSpec(memory_space=pltpu.SMEM)] * len(smem)
    specs += [pl.BlockSpec(memory_space=pltpu.VMEM)] * len(vmem)
    if unread:
        specs[unread] = pl.BlockSpec(memory_space=pl.ANY)
    out_specs = [pl.BlockSpec(memory_space=space)] * len(outs)
    return pl.pallas_call(
        kernel,
        out_shape=[jax.ShapeDtypeStruct(*o) for o in outs],
        in_specs=specs,
        out_specs=out_specs,
        scratch_shapes=scratch,
        compiler_params=pltpu.CompilerParams(vmem_limit_bytes=VMEM),
        cost_estimate=pl.CostEstimate(flops=flops, bytes_accessed=1 << 21, transcendentals=1 << 21),
    )(*smem, *vmem)


def spread(x, axis, n):
    return lax.all_to_all(jnp.broadcast_to(x, (n,) + x.shape), axis, 0, 0)


def gather(x, axis):
    return lax.all_gather(x, axis, axis=0)


def swap(x, axis):
    return lax.ppermute(x, axis, [(0, 1), (1, 0)])


def per_device(
    query_states, key_states, value_states, out_weight, out_grad, doc_lengths, block_order
):
    z_hi = lax.axis_index("z_hi")
    z_lo = lax.axis_index("z2") * 4 + lax.axis_index("z1") * 2 + lax.axis_index("z0")
    at = jnp.stack([z_lo, lax.axis_index("y"), lax.axis_index("core"), z_hi]).astype(jnp.int32)
    smem = (at, block_order, doc_lengths)

    bf16, f32 = jnp.bfloat16, jnp.float32
    weight = out_weight.reshape(4, 2, 512, WIDE)
    send = gather(out_grad, "z_hi")
    kv = jnp.concatenate([key_states, value_states], axis=1)
    send, kv = lax.optimization_barrier((send, kv))
    all_grad = spread(send, "x", 4)
    kv = gather(gather(kv, "z2"), "z1")
    all_grad, kv = lax.optimization_barrier((all_grad, kv))
    grad_attn = jnp.einsum("xzrd,xzdc->rc", all_grad, weight, preferred_element_type=f32)
    send = jnp.concatenate([query_states, grad_attn.astype(bf16)], axis=1)
    send, kv = lax.optimization_barrier((send, kv))
    queries_grads = spread(send, "y", 4)
    kv = gather(kv, "z0").reshape(8, ROWS, WIDE)
    kv, queries_grads = lax.optimization_barrier((kv, queries_grads))
    keys_values = (kv, swap(kv, "core"))
    weight = out_weight.reshape(4, 1024, WIDE)

    partial_out, partial_sums = call(
        forward_kernel,
        [((4, ROWS, WIDE), bf16), ((4, 1, WIDE), f32)],
        [pltpu.VMEM((2048, WIDE), f32), pltpu.VMEM((HD, 2048), bf16)],
        smem,
        (queries_grads,) + keys_values,
        8 * 10**9,
    )
    (send,) = call(
        pack_kernel,
        [((4, ROWS + EXTRA, WIDE), bf16)],
        [],
        (),
        (partial_out, partial_sums, queries_grads),
        10**9,
    )
    order, send = lax.optimization_barrier((block_order, send))
    (plan,) = call(
        plan_kernel,
        [((ROWS,), jnp.int32)],
        [pltpu.SMEM((32,), jnp.int32)],
        (at, order, doc_lengths),
        (),
        3 * 10**9,
        space=pltpu.SMEM,
    )
    parts = lax.all_to_all(send, "y", 0, 0)
    parts, plan = lax.optimization_barrier((parts, plan))
    (terms,) = call(
        combine_kernel,
        [((4, ROWS, 1024), bf16)],
        [pltpu.VMEM((4, 8, WIDE), f32)],
        (at,),
        (parts, weight),
        10**9,
    )
    all_terms = lax.all_to_all(terms, "x", 0, 0)
    dq0, dq1, dq2, dq3, own, far = call(
        backward_kernel,
        [((ROWS, WIDE), bf16)] * 4 + [((4, 2, ROWS, WIDE), bf16)] * 2,
        [
            pltpu.VMEM((2048, HD), f32),
            pltpu.VMEM((2048, HD), f32),
            pltpu.VMEM((2048, HD), bf16),
            pltpu.VMEM((2048, HD), bf16),
            pltpu.VMEM((HD, 2048), bf16),
            pltpu.VMEM((4, 8, WIDE), f32),
            pltpu.VMEM((8, BLOCK, WIDE), bf16),
            pltpu.VMEM((HD, WIDE), f32),
        ],
        (at, plan, doc_lengths),
        (queries_grads.reshape(8, BLOCK, 2 * WIDE), parts, terms) + keys_values,
        12 * 10**9,
        unread=5,
    )
    own, far, all_terms = lax.optimization_barrier((own, far, all_terms))
    far = swap(far, "core")
    both = (own.astype(f32) + far.astype(f32)).astype(bf16)
    both, dq1, dq2, dq3, all_terms = lax.optimization_barrier(
        (both, dq1, dq2, dq3, all_terms)
    )
    partial = [lax.ppermute(x, "y", [(i, i ^ k) for i in range(4)]) for k, x in ((1, dq1), (2, dq2), (3, dq3))]
    both = lax.all_to_all(both, ("z1", "z0"), 0, 0)
    all_terms = jnp.sum(all_terms.astype(f32), axis=0)
    keep = jnp.where(z_hi == 0, all_terms[:, :512], all_terms[:, 512:])
    give = jnp.where(z_hi == 0, all_terms[:, 512:], all_terms[:, :512]).astype(bf16)
    got = swap(give, "z_hi")
    projected = (keep + got.astype(f32)).astype(bf16)
    both, *partial = lax.optimization_barrier((both, *partial))
    dq = dq0.astype(f32)
    for x in partial:
        dq = dq + x.astype(f32)
    grad_query = dq.astype(bf16)
    late = jnp.sum(both[:, 1].astype(f32), axis=0).astype(bf16)
    late = swap(late, "z2")
    stay = jnp.sum(both[:, 0].astype(f32), axis=0)
    grad_kv = (stay + late.astype(f32)).astype(bf16)
    return projected, grad_query, grad_kv[:, :HD], grad_kv[:, HD:]


def solution(mesh):
    fine = Mesh(
        mesh.devices.reshape(2, 2, 2, 4, 2, 4, 2),
        ("z2", "z1", "z0", "y", "core", "x", "z_hi"),
    )
    ctx, head = ("z2", "z1", "z0", "y", "core"), ("x", "z_hi")
    both = P(ctx, head)
    return jax.shard_map(
        per_device,
        mesh=fine,
        in_specs=(both, both, both, P(None, head), both, P(), P()),
        out_specs=(both, both, both, both),
        check_vma=False,
    )
```
